32 devices in a mesh: groups: 2 (over y), expert: 4 (over z), dp: 4 (over x, core).
Axes of the slice: x: 2, y: 2, z: 4, core: 2. Of those that a mesh axis runs over, the one named last changes fastest.
Arguments:
- tokens: bfloat16 [4096, 2048], P(('groups', 'expert', 'dp')), parts along dimension 0, may hold values from -6 to 6
- out_grad: bfloat16 [4096, 2048], P(('groups', 'expert', 'dp')), parts along dimension 0, may hold values from -18 to 18
- route_weight: bfloat16 [4096, 1], P(('groups', 'expert', 'dp')), parts along dimension 0, may hold values from 0.049804688 to 0.5
- expert_ids: int32 [4096, 1], P(('groups', 'expert', 'dp')), parts along dimension 0, may hold values from 0 to 63; in each aligned block of 128 rows (0 to 127, 128 to 255, ...) at most 4 rows name the same one
- gate_weight: bfloat16 [64, 2048, 768], P('expert', None, 'dp'), may hold values from -0.125 to 0.125
- up_weight: bfloat16 [64, 2048, 768], P('expert', None, 'dp'), may hold values from -0.125 to 0.125
- down_weight: bfloat16 [64, 768, 2048], P('expert', 'dp'), may hold values from -0.21875 to 0.21875
Outputs:
- token_grad: bfloat16 [4096, 2048], P(('groups', 'expert', 'dp')), parts along dimension 0
- route_grad: bfloat16 [4096, 1], P(('groups', 'expert', 'dp')), parts along dimension 0
- down_grad: bfloat16 [128, 768, 2048], P(('groups', 'expert'), 'dp'), parts along dimension 0
The draws below stay inside these ranges and needn't reach their ends.
There are 2 independent parts, one for each index of `groups`. The reference program is written for one: setup_inputs(seed, part) draws one part's arguments, and reference() takes and returns one part's arrays. A program takes and returns all parts, laid end to end along the dimension named above; an argument that names none is the same for every part. Nothing has to cross between parts.
Inputs may be any that keep to these rules, and one draw needn't show every extreme that they name: `expert_ids`: each row names 1 different experts; in the rows of one device no expert is named more than 4 times.
All inputs are finite; a program needn't handle non-finite values.
Results may differ from the reference program's by a relative error of at most 0.013.
Values may be sent and summed in bfloat16 or wider, within the bound.
No kernel may reach another device: no remote copies, remote signals or barrier semaphores. Data moves between devices by JAX's collectives and lax.ppermute only.
A program may use at most 576 MiB of HBM per device.

```python
import math
import jax
import jax.numpy as jnp
import numpy as np
from jax import lax

D = 2048
F = 768
E = 64
TOP = 1
TOK_DEV = 128
MOST = 4
FDEV = 192
TOKENS = 2048
N_EXPERT = 4
N_DP = 4


def block_scale(key, shape, split, low, largest):
    def one(axis_at, blocks):
        draws = jax.random.uniform(jax.random.fold_in(jax.random.fold_in(key, 6), axis_at), (blocks,), jnp.float32, low / len(split), largest / len(split))
        return jnp.repeat(jnp.exp(draws), shape[axis_at] // blocks).reshape((-1,) + (1,) * (len(shape) - axis_at - 1))

    level = one(*split[0])
    for cut in split[1:]:
        level = level * one(*cut)
    return level


def assign_block(own_key, own, number, rows, count, top, bound, skew):
    ranking = jax.random.permutation(own_key, count)
    heavy_load, usual = load_shares(count, rows * top, bound, skew, True), load_shares(count, rows * top, bound, skew, False)
    places = jnp.arange(count)

    def named(tallies, turn):
        used = int((tallies > 0).sum())
        fixed = max(1, used // 4)
        passed = fixed + (places - fixed + turn * (used - fixed)) % max(1, count - fixed)
        return jnp.zeros((count,), jnp.int32).at[ranking[jnp.where(places < fixed, places, passed)]].set(jnp.asarray(tallies, jnp.int32))

    tallies = jnp.where(number % 4 == 0, named(heavy_load, number // 4), named(usual, number - number // 4 - 1))
    mixed = jax.random.permutation(jax.random.fold_in(own, 3), count)
    giver, sink = mixed[0:count // 2 * 2:2], mixed[1:count // 2 * 2:2]
    slack = jnp.minimum(tallies[giver] - 1, bound - tallies[sink]) // 2
    slack = jnp.where((giver == ranking[0]) | (sink == ranking[0]) | (tallies[sink] == 0), 0, jnp.maximum(slack, 0))
    passed = jax.random.randint(jax.random.fold_in(own, 4), (count // 2,), 0, 1 << 20) % (slack + 1)
    tallies = tallies.at[giver].add(-passed).at[sink].add(passed)
    members = jnp.searchsorted(jnp.cumsum(tallies), jnp.arange(rows * top), side="right").astype(jnp.int32)
    table = members.reshape(top, rows).T
    table = table[jax.random.permutation(jax.random.fold_in(own, 1), rows)]
    turn = jax.random.randint(jax.random.fold_in(own, 2), (rows, 1), 0, top)
    return jnp.take_along_axis(table, (jnp.arange(top)[None, :] + turn) % top, axis=1)


def load_shares(count, total, limit, skew, full):
    portions = [(1 << 20) // math.isqrt(standing ** skew) + 1 for standing in range(1, count + 1)]
    largest = limit if full else min(limit, max(-(-total // count), total * portions[0] // sum(portions)))
    least = 1 if total - largest >= count - 1 else 0
    holding, rest = [largest] + [least] * (count - 1), total - largest - least * (count - 1)
    while rest > 0:
        free = [i for i in range(1, count) if holding[i] < largest] or [i for i in range(1, count) if holding[i] < limit]
        mass, remaining = sum([portions[i] for i in free]), rest
        for i in free:
            extra = min(limit - holding[i], max(1, remaining * portions[i] // mass), rest)
            holding[i] = holding[i] + extra
            rest = rest - extra
    return np.array(holding)


def bell_draw(rng, shape, width, most, shards=(), kind=jnp.bfloat16):
    values = jax.random.normal(rng, shape, jnp.float32) * width
    if len(shards) > 0:
        values = block_scale(rng, shape, shards, -0.22, 0.18) * values
    return jnp.clip(values, min=-most, max=most).astype(kind)


def setup_inputs(seed: int = 0, part: int = 0) -> dict:
    key_list = jax.random.split(jax.random.key(seed), 8)
    own_keys = jax.random.split(jax.random.fold_in(key_list[7], part), 8)
    tokens = bell_draw(own_keys[0], (TOKENS, D), 1.0, 6.0, ((0, 16),))
    out_grad = bell_draw(own_keys[1], (TOKENS, D), 3.0, 18.0, ((0, 16),))
    route_weight = jnp.clip(jnp.exp(math.log(0.5) - 2.306499 * jax.random.uniform(own_keys[2], (TOKENS, TOP), jnp.float32) ** block_scale(own_keys[2], (TOKENS, TOP), ((0, 16),), -0.2, 0.2)), 0.049804688, 0.5).astype(jnp.bfloat16)
    expert_ids_keys = jax.random.split(jax.random.fold_in(own_keys[3], 1), TOKENS // TOK_DEV)
    expert_ids_turns = jax.random.permutation(jax.random.fold_in(own_keys[3], 3), TOKENS // TOK_DEV)
    expert_ids = jax.vmap(lambda own, number: assign_block(jax.random.fold_in(own_keys[3], 2), own, number, TOK_DEV, E, TOP, MOST, 2))(expert_ids_keys, expert_ids_turns).reshape((TOKENS, TOP))
    gate_weight = bell_draw(key_list[4], (E, D, F), D ** -0.5, 0.125, ((0, 4), (2, 4)))
    up_weight = bell_draw(key_list[5], (E, D, F), D ** -0.5, 0.125, ((0, 4), (2, 4)))
    down_weight = bell_draw(key_list[6], (E, F, D), F ** -0.5, 0.21875, ((0, 4), (1, 4)))
    return dict(tokens=tokens, out_grad=out_grad, route_weight=route_weight, expert_ids=expert_ids, gate_weight=gate_weight, up_weight=up_weight, down_weight=down_weight)


def silu_pair(pre_act):
    sigma_val = jax.nn.sigmoid(pre_act)
    return pre_act * sigma_val, sigma_val * (1.0 + pre_act * (1.0 - sigma_val))


def expert_block(x_block, cot_block, wgt_block, gate_c, up_c, down_c):
    gate_pre = jnp.dot(x_block, gate_c, preferred_element_type=jnp.float32)
    up_pre = jnp.dot(x_block, up_c, preferred_element_type=jnp.float32)
    act_val, act_slope = silu_pair(gate_pre)
    hidden = (act_val * up_pre).astype(jnp.bfloat16)
    out_part = jnp.dot(hidden, down_c, preferred_element_type=jnp.float32)
    weight_part = jnp.sum(cot_block.astype(jnp.float32) * out_part, axis=1)
    scaled = (wgt_block.astype(jnp.float32)[:, None] * cot_block.astype(jnp.float32)).astype(jnp.bfloat16)
    hidden_grad = lax.dot_general(scaled, down_c, (((1,), (1,)), ((), ())), preferred_element_type=jnp.float32)
    down_part = lax.dot_general(hidden, scaled, (((0,), (0,)), ((), ())), preferred_element_type=jnp.float32)
    gate_back = (hidden_grad * up_pre * act_slope).astype(jnp.bfloat16)
    up_back = (hidden_grad * act_val).astype(jnp.bfloat16)
    input_part = lax.dot_general(gate_back, gate_c, (((1,), (1,)), ((), ())), preferred_element_type=jnp.float32)
    input_part = input_part + lax.dot_general(up_back, up_c, (((1,), (1,)), ((), ())), preferred_element_type=jnp.float32)
    return input_part, weight_part, down_part


def rounded(values):
    return lax.optimization_barrier(values.astype(jnp.bfloat16)).astype(jnp.float32)


def reference(tokens, out_grad, route_weight, expert_ids, gate_weight, up_weight, down_weight):
    flat_ids = expert_ids.reshape(-1)
    sorted_at = jnp.argsort(flat_ids, stable=True).astype(jnp.int32)
    counts = jnp.sum((flat_ids[:, None] == jnp.arange(E, dtype=jnp.int32)[None, :]).astype(jnp.int32), axis=0)
    starts = (jnp.cumsum(counts) - counts).astype(jnp.int32)
    room_rows = MOST * N_EXPERT * N_DP
    sorted_at = jnp.concatenate([sorted_at, jnp.zeros((room_rows,), jnp.int32)])
    weight_flat = route_weight.reshape(-1)

    def one_expert(carry, packed):
        input_acc, route_acc = carry
        expert, gate_e, up_e, down_e = packed
        route_at = lax.dynamic_slice_in_dim(sorted_at, starts[expert], room_rows)
        live_row = jnp.arange(room_rows) < counts[expert]
        token_at = route_at // TOP
        rows_x = jnp.where(live_row[:, None], tokens[token_at], jnp.zeros((), jnp.bfloat16))
        cot_rows = jnp.where(live_row[:, None], out_grad[token_at], jnp.zeros((), jnp.bfloat16))
        wgt_rows = jnp.where(live_row, weight_flat[route_at], jnp.zeros((), jnp.bfloat16))
        input_sum = jnp.zeros((room_rows, D), jnp.float32)
        route_sum = jnp.zeros((room_rows,), jnp.float32)
        down_parts = []
        for quarter in range(N_DP):
            low_col = quarter * FDEV
            result = expert_block(rows_x, cot_rows, wgt_rows, gate_e[:, low_col:low_col + FDEV],
                                  up_e[:, low_col:low_col + FDEV], down_e[low_col:low_col + FDEV, :])
            input_sum = input_sum + rounded(result[0])
            route_sum = route_sum + rounded(result[1])
            down_parts.append(result[2])
        input_acc = input_acc.at[token_at].add(rounded(input_sum))
        route_acc = route_acc.at[route_at].add(rounded(route_sum))
        return (input_acc, route_acc), jnp.concatenate(down_parts, axis=0).astype(jnp.bfloat16)

    start_carry = (jnp.zeros((TOKENS, D), jnp.float32), jnp.zeros((TOKENS * TOP,), jnp.float32))
    (input_acc, route_acc), down_g = lax.scan(
        one_expert, start_carry, (jnp.arange(E, dtype=jnp.int32), gate_weight, up_weight, down_weight))
    return (input_acc.astype(jnp.bfloat16), route_acc.reshape(TOKENS, TOP).astype(jnp.bfloat16), down_g)
```

```python
import functools

import jax
import jax.numpy as jnp
from jax import lax
from jax.experimental import pallas as pl
from jax.experimental.pallas import tpu as pltpu
from jax.sharding import PartitionSpec as P

MOST = 4
META = 128
BF = jnp.bfloat16
F32 = jnp.float32
VMEM_BYTES = 48 * 1024 * 1024


def dot_nn(a, b):
    return jnp.dot(a, b, preferred_element_type=F32)


def dot_nt(a, b):
    return lax.dot_general(a, b, (((1,), (1,)), ((), ())), preferred_element_type=F32)


def dot_tn(a, b):
    return lax.dot_general(a, b, (((0,), (0,)), ((), ())), preferred_element_type=F32)


def params():
    return pltpu.CompilerParams(vmem_limit_bytes=VMEM_BYTES)


def cost(flops, moved):
    return pl.CostEstimate(flops=int(flops), bytes_accessed=int(moved), transcendentals=0)


def whole(array):
    zeros = (0,) * array.ndim
    return pl.BlockSpec(array.shape, lambda *_: zeros)


def route_columns(ids, per_device):
    count = ids.shape[0]
    across = jnp.broadcast_to(ids.astype(F32), (count, count))
    down = jnp.transpose(across)
    row = lax.broadcasted_iota(jnp.int32, (count, count), 0)
    col = lax.broadcasted_iota(jnp.int32, (count, count), 1)
    earlier = col < row
    inv = 1.0 / per_device
    same_expert = jnp.where((across == down) & earlier, 1.0, 0.0)
    same_shard = jnp.where(
        (jnp.floor((across + 0.5) * inv) == jnp.floor((down + 0.5) * inv)) & earlier, 1.0, 0.0
    )
    rank = jnp.sum(same_expert, axis=1, keepdims=True)
    place = jnp.sum(same_shard, axis=1, keepdims=True)
    shard = jnp.floor((ids.astype(F32) + 0.5) * inv)
    local = ids.astype(F32) - shard * per_device
    return shard, local, rank, place


def slot_table(ids, per_device, room, n_shards):
    shard, local, rank, place = route_columns(ids, per_device)
    slot = jnp.where(place < room, shard * room + place, -1.0).astype(jnp.int32)
    lanes = lax.broadcasted_iota(jnp.int32, (ids.shape[0], n_shards * room), 1)
    return jnp.where(lanes == slot, 1.0, 0.0).astype(BF), local * MOST + rank + 1.0


def pack_kernel(per_device, room, n_shards, ids_ref, tok_ref, cot_ref, wgt_ref, x_ref, c_ref):
    table, tag = slot_table(ids_ref[...], per_device, room, n_shards)
    width = tok_ref.shape[1]
    x_ref[:, :width] = dot_tn(table, tok_ref[...]).astype(BF)
    lane = lax.broadcasted_iota(jnp.int32, (tag.shape[0], META), 1)
    info = jnp.where(lane == 0, tag, jnp.where(lane == 1, wgt_ref[...].astype(F32), 0.0))
    x_ref[:, width:] = dot_tn(table, info.astype(BF)).astype(BF)
    c_ref[...] = dot_tn(table, cot_ref[...]).astype(BF)


def pack_rows(ids, tokens, out_grad, wgt, per_device, room, n_shards):
    rows, width = n_shards * room, tokens.shape[1]
    args = (ids, tokens, out_grad, wgt)
    return pl.pallas_call(
        functools.partial(pack_kernel, per_device, room, n_shards),
        grid=(1,),
        in_specs=[whole(a) for a in args],
        out_specs=[
            pl.BlockSpec((rows, width + META), lambda i: (0, 0)),
            pl.BlockSpec((rows, width), lambda i: (0, 0)),
        ],
        out_shape=[
            jax.ShapeDtypeStruct((rows, width + META), BF),
            jax.ShapeDtypeStruct((rows, width), BF),
        ],
        compiler_params=params(),
        cost_estimate=cost(4e8, 4e6),
        name="pack_rows",
    )(*args)


def sorted_table(meta, room, n_shards, n_sorted):
    tag = meta[:, 0:1].astype(F32).astype(jnp.int32)
    rows = lax.broadcasted_iota(jnp.int32, tag.shape, 0)
    source = jnp.floor((rows.astype(F32) + 0.5) * (1.0 / room)).astype(jnp.int32)
    at = tag - 1
    local = at // MOST
    dest = local * (n_shards * MOST) + source * MOST + (at - local * MOST)
    dest = jnp.where(tag > 0, dest, -1)
    lanes = lax.broadcasted_iota(jnp.int32, (meta.shape[0], n_sorted), 1)
    return jnp.where(lanes == dest, 1.0, 0.0).astype(BF)


def spread(table, rows_ref, width, out_ref, member, chunk=512):
    experts, _, _ = out_ref.shape
    per_expert = table.shape[1] // experts
    turned = jnp.transpose(table)
    low = member * per_expert
    for c in range(0, width, chunk):
        part = dot_nn(turned, rows_ref[:, c : c + chunk]).astype(BF)
        out_ref[:, low : low + per_expert, c : c + chunk] = part.reshape(
            experts, per_expert, chunk
        )


def first_kernel(n_dp, room, n_shards, *refs):
    x_refs = refs[:n_dp]
    gate_ref, up_ref, g_ref, u_ref, xs = refs[n_dp:]
    experts, expert_rows, width = xs.shape
    n_sorted = experts * expert_rows // n_dp

    @pl.when(pl.program_id(0) == 0)
    def _():
        for d in range(n_dp):
            table = sorted_table(x_refs[d][:, width : width + META], room, n_shards, n_sorted)
            spread(table, x_refs[d], width, xs, d)

    x_block = xs[pl.program_id(0)]
    g_ref[0] = dot_nt(x_block, gate_ref[0])
    u_ref[0] = dot_nt(x_block, up_ref[0])


def first_layer(x_list, gate, up, room, n_shards):
    n_dp = len(x_list)
    experts, hidden, width = gate.shape
    expert_rows = n_dp * n_shards * MOST
    by_expert = lambda e: (e, 0, 0)
    shape = jax.ShapeDtypeStruct((experts, expert_rows, hidden), F32)
    return pl.pallas_call(
        functools.partial(first_kernel, n_dp, room, n_shards),
        grid=(experts,),
        in_specs=[whole(x) for x in x_list]
        + [pl.BlockSpec((1, hidden, width), by_expert)] * 2,
        out_specs=[pl.BlockSpec((1, expert_rows, hidden), by_expert)] * 2,
        out_shape=[shape, shape],
        scratch_shapes=[pltpu.VMEM((experts, expert_rows, width), BF)],
        compiler_params=params(),
        cost_estimate=cost(2e9, 3e7),
        name="gate_up",
    )(*x_list, gate, up)


def second_kernel(n_dp, room, n_shards, *refs):
    m_refs, c_refs = refs[:n_dp], refs[n_dp : 2 * n_dp]
    g_ref, u_ref, down_ref, dg_ref, du_ref, hw_ref, cs_ref, r_ref, cs, ms = refs[2 * n_dp :]
    experts, expert_rows, width = cs.shape
    n_sorted = experts * expert_rows // n_dp

    @pl.when(pl.program_id(0) == 0)
    def _():
        for d in range(n_dp):
            meta = m_refs[d][...]
            table = sorted_table(meta, room, n_shards, n_sorted)
            spread(table, c_refs[d], width, cs, d)
            spread(table, m_refs[d], META, ms, d, META)

    at = pl.program_id(0)
    c_block = cs[at]
    cs_ref[0] = c_block
    weight = ms[at][:, 1:2].astype(F32)
    back = dot_nt(c_block, down_ref[0])
    g, u = g_ref[0], u_ref[0]
    sig = jax.nn.sigmoid(g)
    act = g * sig
    hidden = act * u
    router = jnp.sum(hidden.astype(BF).astype(F32) * back, axis=1, keepdims=True)
    r_ref[0] = jnp.broadcast_to(router, (expert_rows, META)).astype(BF)
    hw_ref[0] = (hidden * weight).astype(BF)
    scaled = back * weight
    dg_ref[0] = (scaled * u * (sig * (1.0 + g * (1.0 - sig)))).astype(BF)
    du_ref[0] = (scaled * act).astype(BF)


def second_layer(x_list, c_list, g, u, down, room, n_shards):
    n_dp = len(c_list)
    experts, hidden, width = down.shape
    expert_rows = g.shape[1]
    slots = c_list[0].shape[0]
    by_expert = lambda e: (e, 0, 0)
    small = jax.ShapeDtypeStruct((experts, expert_rows, hidden), BF)
    small_spec = pl.BlockSpec((1, expert_rows, hidden), by_expert)
    return pl.pallas_call(
        functools.partial(second_kernel, n_dp, room, n_shards),
        grid=(experts,),
        in_specs=[pl.BlockSpec((slots, META), lambda e: (0, width // META))] * n_dp
        + [whole(c) for c in c_list]
        + [small_spec] * 2
        + [pl.BlockSpec((1, hidden, width), by_expert)],
        out_specs=[small_spec] * 3
        + [
            pl.BlockSpec((1, expert_rows, width), by_expert),
            pl.BlockSpec((1, expert_rows, META), by_expert),
        ],
        out_shape=[small] * 3
        + [
            jax.ShapeDtypeStruct((experts, expert_rows, width), BF),
            jax.ShapeDtypeStruct((experts, expert_rows, META), BF),
        ],
        scratch_shapes=[
            pltpu.VMEM((experts, expert_rows, width), BF),
            pltpu.VMEM((experts, expert_rows, META), BF),
        ],
        compiler_params=params(),
        cost_estimate=cost(2e9, 2e7),
        name="hidden_grads",
    )(*x_list, *c_list, g, u, down)


def third_kernel(n_dp, room, n_shards, with_router, *refs):
    m_refs = refs[:n_dp]
    rest = refs[n_dp:]
    dg_ref, du_ref, gate_ref, up_ref = rest[:4]
    rest = rest[4:]
    if with_router:
        r_ref, rest = rest[0], rest[1:]
    out_refs, acc = rest[:n_dp], rest[n_dp]
    experts, expert_rows = pl.num_programs(0), dg_ref.shape[1]
    _, _, per_expert, width = acc.shape
    part = gate_ref.shape[2]
    at = pl.program_id(0)
    grad = dot_nn(dg_ref[0], gate_ref[0]) + dot_nn(du_ref[0], up_ref[0])
    grad = grad.astype(BF)
    for d in range(n_dp):
        low = d * per_expert
        acc[d, at, :, :part] = grad[low : low + per_expert]
        if with_router:
            acc[d, at, :, part:] = r_ref[0, low : low + per_expert]

    @pl.when(at == acc.shape[1] - 1)
    def _():
        for d in range(n_dp):
            table = sorted_table(m_refs[d][...], room, n_shards, acc.shape[1] * per_expert)
            rows = acc[d].reshape(acc.shape[1] * per_expert, width)
            out_refs[d][...] = dot_nn(table, rows).astype(BF)


def third_layer(x_list, dg, du, gate, up, router, half, n_half, room, n_shards):
    n_dp = len(x_list)
    experts, hidden, full = gate.shape
    expert_rows = dg.shape[1]
    slots = x_list[0].shape[0]
    part = full // n_half
    width = part + (0 if router is None else META)
    by_expert = lambda e: (e, 0, 0)
    small_spec = pl.BlockSpec((1, expert_rows, hidden), by_expert)
    weight_spec = pl.BlockSpec((1, hidden, part), lambda e: (e, 0, half))
    args = [*x_list, dg, du, gate, up]
    specs = [pl.BlockSpec((slots, META), lambda e: (0, full // META))] * n_dp
    specs += [small_spec] * 2 + [weight_spec] * 2
    if router is not None:
        args.append(router)
        specs.append(pl.BlockSpec((1, expert_rows, META), by_expert))
    return pl.pallas_call(
        functools.partial(third_kernel, n_dp, room, n_shards, router is not None),
        grid=(experts,),
        in_specs=specs,
        out_specs=[pl.BlockSpec((slots, width), lambda e: (0, 0))] * n_dp,
        out_shape=[jax.ShapeDtypeStruct((slots, width), BF)] * n_dp,
        scratch_shapes=[pltpu.VMEM((n_dp, experts, expert_rows // n_dp, width), BF)],
        compiler_params=params(),
        cost_estimate=cost(1e9, 1.5e7),
        name="input_grads",
    )(*args)


def down_kernel(hw_ref, cs_ref, out_ref):
    out_ref[0] = dot_tn(hw_ref[0], cs_ref[0]).astype(BF)


def down_layer(hw, cs):
    experts, rows, hidden = hw.shape
    width = cs.shape[2]
    by_expert = lambda e: (e, 0, 0)
    return pl.pallas_call(
        down_kernel,
        grid=(experts,),
        in_specs=[
            pl.BlockSpec((1, rows, hidden), by_expert),
            pl.BlockSpec((1, rows, width), by_expert),
        ],
        out_specs=pl.BlockSpec((1, hidden, width), by_expert),
        out_shape=jax.ShapeDtypeStruct((experts, hidden, width), BF),
        compiler_params=params(),
        cost_estimate=cost(1e9, 1.8e7),
        name="down_grads",
    )(hw, cs)


def home_kernel(per_device, room, n_shards, n_half, n_blocks, ids_ref, *refs):
    table, _ = slot_table(ids_ref[...], per_device, room, n_shards)
    blocks, (tok_ref, route_ref) = refs[:-2], refs[-2:]
    part = tok_ref.shape[1] // n_half
    size = n_shards * room // n_blocks
    for h in range(n_half):
        total = None
        for k in range(n_blocks):
            term = dot_nn(table[:, k * size : (k + 1) * size], blocks[h * n_blocks + k][...])
            total = term if total is None else total + term
        tok_ref[:, h * part : (h + 1) * part] = total[:, :part].astype(BF)
        if h == n_half - 1:
            route_ref[...] = total[:, part : part + META].astype(BF)


def home_rows(ids, halves, width, per_device, room, n_shards):
    n_half, n_blocks = len(halves), len(halves[0])
    count = ids.shape[0]
    blocks = [b for half in halves for b in half]
    return pl.pallas_call(
        functools.partial(home_kernel, per_device, room, n_shards, n_half, n_blocks),
        grid=(1,),
        in_specs=[whole(ids)] + [whole(b) for b in blocks],
        out_specs=[
            pl.BlockSpec((count, width), lambda i: (0, 0)),
            pl.BlockSpec((count, META), lambda i: (0, 0)),
        ],
        out_shape=[
            jax.ShapeDtypeStruct((count, width), BF),
            jax.ShapeDtypeStruct((count, META), BF),
        ],
        compiler_params=params(),
        cost_estimate=cost(2e8, 2e6),
        name="home_rows",
    )(ids, *blocks)


def shifted(value, axis, step):
    n = lax.axis_size(axis)
    return lax.ppermute(value, axis, [(i, (i + step) % n) for i in range(n)])


def swapped(value, axis, bit):
    n = lax.axis_size(axis)
    return lax.ppermute(value, axis, [(i, i ^ bit) for i in range(n)])


def direct(n_shards):
    return n_shards <= 4


def to_shards(rows, room, n_shards):
    if not direct(n_shards):
        shaped = rows.reshape(n_shards, room, rows.shape[1])
        return lax.all_to_all(shaped, "expert", 0, 0, tiled=True).reshape(rows.shape)
    parts = [rows[:room]]
    for k in range(1, n_shards):
        parts.append(shifted(rows[k * room : (k + 1) * room], "expert", k))
    return jnp.concatenate(parts)


def from_shards(rows, room, n_shards):
    if not direct(n_shards):
        return [to_shards(rows, room, n_shards)]
    parts = [rows[:room]]
    for k in range(1, n_shards):
        parts.append(shifted(rows[k * room : (k + 1) * room], "expert", -k))
    return parts


def dp_bits(n_dp):
    bits, bit = [], 1
    while bit < n_dp:
        bits.append(bit)
        bit *= 2
    return bits


def gather_dp(rows, n_dp):
    got = {0: rows}
    for bit in reversed(dp_bits(n_dp)):
        for k in list(got):
            got[k ^ bit] = swapped(got[k], "dp", bit)
    return [got[k] for k in range(n_dp)]


def scatter_dp(parts, n_dp):
    have = dict(enumerate(parts))
    bits = dp_bits(n_dp)
    for bit in bits:
        left = {}
        for k in sorted(have, reverse=True):
            if k & bit == 0:
                moved = swapped(have[k ^ bit], "dp", bit)
                left[k] = (have[k].astype(F32) + moved.astype(F32)).astype(BF)
        have = left
    return have[0]


def run(room, ids, tokens, out_grad, route_weight, gate, up, down):
    n_shards, n_dp = lax.axis_size("expert"), lax.axis_size("dp")
    per_device, width = gate.shape[0], tokens.shape[1]
    gate, up = jnp.swapaxes(gate, 1, 2), jnp.swapaxes(up, 1, 2)
    send_x, send_c = pack_rows(ids, tokens, out_grad, route_weight, per_device, room, n_shards)
    x_list = gather_dp(to_shards(send_x, room, n_shards), n_dp)
    c_list = gather_dp(to_shards(send_c, room, n_shards), n_dp)
    g, u = first_layer(x_list, gate, up, room, n_shards)
    dg, du, hw, cs, router = second_layer(x_list, c_list, g, u, down, room, n_shards)
    n_half = 2
    halves = []
    for half in range(n_half):
        column = router if half == n_half - 1 else None
        parts = third_layer(
            x_list, dg, du, gate, up, column, half, n_half, room, n_shards
        )
        halves.append(from_shards(scatter_dp(parts, n_dp), room, n_shards))
    down_grad = down_layer(hw, cs)
    token_grad, route = home_rows(ids, halves, width, per_device, room, n_shards)
    return token_grad, route[:, :1], down_grad


def shards(tokens, out_grad, route_weight, expert_ids, gate, up, down):
    n_shards = lax.axis_size("expert")
    per_device = gate.shape[0]
    slot_rows = min(expert_ids.shape[0], per_device * MOST)
    ids = expert_ids
    if direct(n_shards):
        total = n_shards * per_device
        ids = (ids - lax.axis_index("expert") * per_device + total) % total
    return run(slot_rows, ids, tokens, out_grad, route_weight, gate, up, down)


def solution(mesh):
    rows = P(("groups", "expert", "dp"), None)
    in_specs = (
        rows,
        rows,
        rows,
        rows,
        P("expert", None, "dp"),
        P("expert", None, "dp"),
        P("expert", "dp", None),
    )
    out_specs = (rows, rows, P(("groups", "expert"), "dp", None))
    return jax.shard_map(shards, mesh=mesh, in_specs=in_specs, out_specs=out_specs, check_vma=False)
```

```python
import functools

import jax
import jax.numpy as jnp
from jax import lax
from jax.experimental import pallas as pl
from jax.experimental.pallas import tpu as pltpu
from jax.sharding import PartitionSpec as P

MOST = 4
META = 128
OVER = 2
BF = jnp.bfloat16
F32 = jnp.float32
VMEM_BYTES = 48 * 1024 * 1024


def dot_nn(a, b):
    return jnp.dot(a, b, preferred_element_type=F32)


def dot_nt(a, b):
    return lax.dot_general(a, b, (((1,), (1,)), ((), ())), preferred_element_type=F32)


def dot_tn(a, b):
    return lax.dot_general(a, b, (((0,), (0,)), ((), ())), preferred_element_type=F32)


def params():
    return pltpu.CompilerParams(vmem_limit_bytes=VMEM_BYTES)


def cost(flops, moved):
    return pl.CostEstimate(flops=int(flops), bytes_accessed=int(moved), transcendentals=0)


def step_of(experts, most):
    step = 1
    while step * 2 <= most and experts % (step * 2) == 0:
        step *= 2
    return step


def whole(array):
    zeros = (0,) * array.ndim
    return pl.BlockSpec(array.shape, lambda *_: zeros)


def route_columns(ids, per_device):
    count = ids.shape[0]
    across = jnp.broadcast_to(ids.astype(F32), (count, count))
    down = jnp.transpose(across)
    row = lax.broadcasted_iota(jnp.int32, (count, count), 0)
    col = lax.broadcasted_iota(jnp.int32, (count, count), 1)
    earlier = col < row
    inv = 1.0 / per_device
    same_expert = jnp.where((across == down) & earlier, 1.0, 0.0)
    same_shard = jnp.where(
        (jnp.floor((across + 0.5) * inv) == jnp.floor((down + 0.5) * inv)) & earlier, 1.0, 0.0
    )
    rank = jnp.sum(same_expert, axis=1, keepdims=True)
    place = jnp.sum(same_shard, axis=1, keepdims=True)
    shard = jnp.floor((ids.astype(F32) + 0.5) * inv)
    local = ids.astype(F32) - shard * per_device
    return shard, local, rank, place


def slot_table(ids, per_device, room, n_shards):
    shard, local, rank, place = route_columns(ids, per_device)
    slot = jnp.where(place < room, shard * room + place, -1.0).astype(jnp.int32)
    lanes = lax.broadcasted_iota(jnp.int32, (ids.shape[0], n_shards * room), 1)
    over = jnp.max(place, axis=0, keepdims=True) >= room
    return jnp.where(lanes == slot, 1.0, 0.0).astype(BF), local * MOST + rank + 1.0, over


def pack_kernel(per_device, room, n_shards, ids_ref, tok_ref, cot_ref, wgt_ref, x_ref, c_ref):
    table, tag, over = slot_table(ids_ref[...], per_device, room, n_shards)
    width = tok_ref.shape[1]
    x_ref[:, :width] = dot_tn(table, tok_ref[...]).astype(BF)
    lane = lax.broadcasted_iota(jnp.int32, (tag.shape[0], META), 1)
    info = jnp.where(lane == 0, tag, jnp.where(lane == 1, wgt_ref[...].astype(F32), 0.0))
    packed = dot_tn(table, info.astype(BF))
    lane = lax.broadcasted_iota(jnp.int32, packed.shape, 1)
    flag = jnp.broadcast_to(jnp.where(over, 1.0, 0.0), packed.shape)
    x_ref[:, width:] = jnp.where(lane == OVER, flag, packed).astype(BF)
    c_ref[...] = dot_tn(table, cot_ref[...]).astype(BF)


def pack_rows(ids, tokens, out_grad, wgt, per_device, room, n_shards):
    rows, width = n_shards * room, tokens.shape[1]
    args = (ids, tokens, out_grad, wgt)
    return pl.pallas_call(
        functools.partial(pack_kernel, per_device, room, n_shards),
        grid=(1,),
        in_specs=[whole(a) for a in args],
        out_specs=[
            pl.BlockSpec((rows, width + META), lambda i: (0, 0)),
            pl.BlockSpec((rows, width), lambda i: (0, 0)),
        ],
        out_shape=[
            jax.ShapeDtypeStruct((rows, width + META), BF),
            jax.ShapeDtypeStruct((rows, width), BF),
        ],
        compiler_params=params(),
        cost_estimate=cost(4e8, 4e6),
        name="pack_rows",
    )(*args)


def sorted_table(meta, room, n_shards, n_sorted):
    tag = meta[:, 0:1].astype(F32).astype(jnp.int32)
    rows = lax.broadcasted_iota(jnp.int32, tag.shape, 0)
    source = jnp.floor((rows.astype(F32) + 0.5) * (1.0 / room)).astype(jnp.int32)
    at = tag - 1
    local = at // MOST
    dest = local * (n_shards * MOST) + source * MOST + (at - local * MOST)
    dest = jnp.where(tag > 0, dest, -1)
    lanes = lax.broadcasted_iota(jnp.int32, (meta.shape[0], n_sorted), 1)
    return jnp.where(lanes == dest, 1.0, 0.0).astype(BF)


def spread(table, rows_ref, width, out_ref, member, chunk=512):
    experts, _, _ = out_ref.shape
    per_expert = table.shape[1] // experts
    turned = jnp.transpose(table)
    low = member * per_expert
    for c in range(0, width, chunk):
        part = dot_nn(turned, rows_ref[:, c : c + chunk]).astype(BF)
        out_ref[:, low : low + per_expert, c : c + chunk] = part.reshape(
            experts, per_expert, chunk
        )


def first_kernel(n_dp, room, n_shards, *refs):
    x_refs = refs[:n_dp]
    gate_ref, up_ref, g_ref, u_ref, xs = refs[n_dp:]
    experts, expert_rows, width = xs.shape
    n_sorted = experts * expert_rows // n_dp

    @pl.when(pl.program_id(0) == 0)
    def _():
        for d in range(n_dp):
            table = sorted_table(x_refs[d][:, width : width + META], room, n_shards, n_sorted)
            spread(table, x_refs[d], width, xs, d)

    step = gate_ref.shape[0]
    for i in range(step):
        x_block = xs[pl.program_id(0) * step + i]
        g_ref[i] = dot_nt(x_block, gate_ref[i])
        u_ref[i] = dot_nt(x_block, up_ref[i])


def first_layer(x_list, gate, up, room, n_shards):
    n_dp = len(x_list)
    experts, hidden, width = gate.shape
    expert_rows = n_dp * n_shards * MOST
    step = step_of(experts, 4)
    by_expert = lambda e: (e, 0, 0)
    shape = jax.ShapeDtypeStruct((experts, expert_rows, hidden), F32)
    return pl.pallas_call(
        functools.partial(first_kernel, n_dp, room, n_shards),
        grid=(experts // step,),
        in_specs=[whole(x) for x in x_list]
        + [pl.BlockSpec((step, hidden, width), by_expert)] * 2,
        out_specs=[pl.BlockSpec((step, expert_rows, hidden), by_expert)] * 2,
        out_shape=[shape, shape],
        scratch_shapes=[pltpu.VMEM((experts, expert_rows, width), BF)],
        compiler_params=params(),
        cost_estimate=cost(2e9, 3e7),
        name="gate_up",
    )(*x_list, gate, up)


def second_kernel(n_dp, room, n_shards, *refs):
    m_refs, c_refs = refs[:n_dp], refs[n_dp : 2 * n_dp]
    g_ref, u_ref, down_ref, dg_ref, du_ref, hw_ref, cs_ref, r_ref, cs, ms = refs[2 * n_dp :]
    experts, expert_rows, width = cs.shape
    n_sorted = experts * expert_rows // n_dp

    @pl.when(pl.program_id(0) == 0)
    def _():
        for d in range(n_dp):
            meta = m_refs[d][...]
            table = sorted_table(meta, room, n_shards, n_sorted)
            spread(table, c_refs[d], width, cs, d)
            spread(table, m_refs[d], META, ms, d, META)

    step = g_ref.shape[0]
    for i in range(step):
        at = pl.program_id(0) * step + i
        c_block = cs[at]
        cs_ref[i] = c_block
        weight = ms[at][:, 1:2].astype(F32)
        back = dot_nt(c_block, down_ref[i])
        g, u = g_ref[i], u_ref[i]
        sig = jax.nn.sigmoid(g)
        act = g * sig
        hidden = act * u
        router = jnp.sum(hidden.astype(BF).astype(F32) * back, axis=1, keepdims=True)
        r_ref[i] = jnp.broadcast_to(router, (expert_rows, META)).astype(BF)
        hw_ref[i] = (hidden * weight).astype(BF)
        scaled = back * weight
        dg_ref[i] = (scaled * u * (sig * (1.0 + g * (1.0 - sig)))).astype(BF)
        du_ref[i] = (scaled * act).astype(BF)


def second_layer(x_list, c_list, g, u, down, room, n_shards):
    n_dp = len(c_list)
    experts, hidden, width = down.shape
    expert_rows = g.shape[1]
    slots = c_list[0].shape[0]
    step = step_of(experts, 4)
    by_expert = lambda e: (e, 0, 0)
    small = jax.ShapeDtypeStruct((experts, expert_rows, hidden), BF)
    small_spec = pl.BlockSpec((step, expert_rows, hidden), by_expert)
    return pl.pallas_call(
        functools.partial(second_kernel, n_dp, room, n_shards),
        grid=(experts // step,),
        in_specs=[pl.BlockSpec((slots, META), lambda e: (0, width // META))] * n_dp
        + [whole(c) for c in c_list]
        + [small_spec] * 2
        + [pl.BlockSpec((step, hidden, width), by_expert)],
        out_specs=[small_spec] * 3
        + [
            pl.BlockSpec((step, expert_rows, width), by_expert),
            pl.BlockSpec((step, expert_rows, META), by_expert),
        ],
        out_shape=[small] * 3
        + [
            jax.ShapeDtypeStruct((experts, expert_rows, width), BF),
            jax.ShapeDtypeStruct((experts, expert_rows, META), BF),
        ],
        scratch_shapes=[
            pltpu.VMEM((experts, expert_rows, width), BF),
            pltpu.VMEM((experts, expert_rows, META), BF),
        ],
        compiler_params=params(),
        cost_estimate=cost(2e9, 2e7),
        name="hidden_grads",
    )(*x_list, *c_list, g, u, down)


def third_kernel(n_dp, room, n_shards, with_router, *refs):
    m_refs = refs[:n_dp]
    rest = refs[n_dp:]
    dg_ref, du_ref, gate_ref, up_ref = rest[:4]
    rest = rest[4:]
    if with_router:
        r_ref, rest = rest[0], rest[1:]
    out_refs, acc = rest[:n_dp], rest[n_dp]
    _, experts, per_expert, width = acc.shape
    step, _, part = gate_ref.shape
    for i in range(step):
        at = pl.program_id(0) * step + i
        grad = (dot_nn(dg_ref[i], gate_ref[i]) + dot_nn(du_ref[i], up_ref[i])).astype(BF)
        for d in range(n_dp):
            low = d * per_expert
            acc[d, at, :, :part] = grad[low : low + per_expert]
            if with_router:
                acc[d, at, :, part:] = r_ref[i, low : low + per_expert]

    @pl.when(pl.program_id(0) == pl.num_programs(0) - 1)
    def _():
        for d in range(n_dp):
            table = sorted_table(m_refs[d][...], room, n_shards, experts * per_expert)
            rows = acc[d].reshape(experts * per_expert, width)
            out_refs[d][...] = dot_nn(table, rows).astype(BF)


def third_layer(x_list, dg, du, gate, up, router, half, n_half, room, n_shards):
    n_dp = len(x_list)
    experts, hidden, full = gate.shape
    expert_rows = dg.shape[1]
    slots = x_list[0].shape[0]
    part = full // n_half
    width = part + (0 if router is None else META)
    step = step_of(experts, 4)
    by_expert = lambda e: (e, 0, 0)
    small_spec = pl.BlockSpec((step, expert_rows, hidden), by_expert)
    weight_spec = pl.BlockSpec((step, hidden, part), lambda e: (e, 0, half))
    args = [*x_list, dg, du, gate, up]
    specs = [pl.BlockSpec((slots, META), lambda e: (0, full // META))] * n_dp
    specs += [small_spec] * 2 + [weight_spec] * 2
    if router is not None:
        args.append(router)
        specs.append(pl.BlockSpec((step, expert_rows, META), by_expert))
    return pl.pallas_call(
        functools.partial(third_kernel, n_dp, room, n_shards, router is not None),
        grid=(experts // step,),
        in_specs=specs,
        out_specs=[pl.BlockSpec((slots, width), lambda e: (0, 0))] * n_dp,
        out_shape=[jax.ShapeDtypeStruct((slots, width), BF)] * n_dp,
        scratch_shapes=[pltpu.VMEM((n_dp, experts, expert_rows // n_dp, width), BF)],
        compiler_params=params(),
        cost_estimate=cost(1e9, 1.5e7),
        name="input_grads",
    )(*args)


def down_kernel(hw_ref, cs_ref, out_ref):
    for i in range(hw_ref.shape[0]):
        out_ref[i] = dot_tn(hw_ref[i], cs_ref[i]).astype(BF)


def down_layer(hw, cs):
    experts, rows, hidden = hw.shape
    width = cs.shape[2]
    step = step_of(experts, 4)
    by_expert = lambda e: (e, 0, 0)
    return pl.pallas_call(
        down_kernel,
        grid=(experts // step,),
        in_specs=[
            pl.BlockSpec((step, rows, hidden), by_expert),
            pl.BlockSpec((step, rows, width), by_expert),
        ],
        out_specs=pl.BlockSpec((step, hidden, width), by_expert),
        out_shape=jax.ShapeDtypeStruct((experts, hidden, width), BF),
        compiler_params=params(),
        cost_estimate=cost(1e9, 1.8e7),
        name="down_grads",
    )(hw, cs)


def home_kernel(per_device, room, n_shards, n_half, n_blocks, ids_ref, *refs):
    table, _, _ = slot_table(ids_ref[...], per_device, room, n_shards)
    blocks, (tok_ref, route_ref) = refs[:-2], refs[-2:]
    part = tok_ref.shape[1] // n_half
    size = n_shards * room // n_blocks
    for h in range(n_half):
        total = None
        for k in range(n_blocks):
            term = dot_nn(table[:, k * size : (k + 1) * size], blocks[h * n_blocks + k][...])
            total = term if total is None else total + term
        tok_ref[:, h * part : (h + 1) * part] = total[:, :part].astype(BF)
        if h == n_half - 1:
            route_ref[...] = total[:, part : part + META].astype(BF)


def home_rows(ids, halves, width, per_device, room, n_shards):
    n_half, n_blocks = len(halves), len(halves[0])
    count = ids.shape[0]
    blocks = [b for half in halves for b in half]
    return pl.pallas_call(
        functools.partial(home_kernel, per_device, room, n_shards, n_half, n_blocks),
        grid=(1,),
        in_specs=[whole(ids)] + [whole(b) for b in blocks],
        out_specs=[
            pl.BlockSpec((count, width), lambda i: (0, 0)),
            pl.BlockSpec((count, META), lambda i: (0, 0)),
        ],
        out_shape=[
            jax.ShapeDtypeStruct((count, width), BF),
            jax.ShapeDtypeStruct((count, META), BF),
        ],
        compiler_params=params(),
        cost_estimate=cost(2e8, 2e6),
        name="home_rows",
    )(ids, *blocks)


def shifted(value, axis, step):
    n = lax.axis_size(axis)
    return lax.ppermute(value, axis, [(i, (i + step) % n) for i in range(n)])


def swapped(value, axis, bit):
    n = lax.axis_size(axis)
    return lax.ppermute(value, axis, [(i, i ^ bit) for i in range(n)])


def direct(n_shards):
    return n_shards <= 4


def to_shards(rows, room, n_shards):
    if not direct(n_shards):
        shaped = rows.reshape(n_shards, room, rows.shape[1])
        return lax.all_to_all(shaped, "expert", 0, 0, tiled=True).reshape(rows.shape)
    parts = [rows[:room]]
    for k in range(1, n_shards):
        parts.append(shifted(rows[k * room : (k + 1) * room], "expert", k))
    return jnp.concatenate(parts)


def from_shards(rows, room, n_shards):
    if not direct(n_shards):
        return [to_shards(rows, room, n_shards)]
    parts = [rows[:room]]
    for k in range(1, n_shards):
        parts.append(shifted(rows[k * room : (k + 1) * room], "expert", -k))
    return parts


def dp_bits(n_dp):
    bits, bit = [], 1
    while bit < n_dp:
        bits.append(bit)
        bit *= 2
    return bits


def gather_dp(rows, n_dp):
    got = {0: rows}
    for bit in reversed(dp_bits(n_dp)):
        for k in list(got):
            got[k ^ bit] = swapped(got[k], "dp", bit)
    return [got[k] for k in range(n_dp)]


def scatter_dp(parts, n_dp):
    have = dict(enumerate(parts))
    bits = dp_bits(n_dp)
    for bit in bits:
        left = {}
        for k in sorted(have, reverse=True):
            if k & bit == 0:
                moved = swapped(have[k ^ bit], "dp", bit)
                left[k] = (have[k].astype(F32) + moved.astype(F32)).astype(BF)
        have = left
    return have[0]


def begin(room, ids, tokens, out_grad, route_weight, per_device):
    n_shards = lax.axis_size("expert")
    send_x, send_c = pack_rows(ids, tokens, out_grad, route_weight, per_device, room, n_shards)
    own_x = to_shards(send_x, room, n_shards)
    send_c, own_x = lax.optimization_barrier((send_c, own_x))
    return own_x, to_shards(send_c, room, n_shards)


def finish(room, ids, x_list, own_c, gate, up, down):
    n_shards, n_dp = lax.axis_size("expert"), lax.axis_size("dp")
    per_device, width = gate.shape[0], down.shape[2]
    c_list = gather_dp(own_c, n_dp)
    g, u = first_layer(x_list, gate, up, room, n_shards)
    dg, du, hw, cs, router = second_layer(x_list, c_list, g, u, down, room, n_shards)
    n_half = 2
    halves = []
    for half in range(n_half):
        column = router if half == n_half - 1 else None
        parts = third_layer(
            x_list, dg, du, gate, up, column, half, n_half, room, n_shards
        )
        halves.append(from_shards(scatter_dp(parts, n_dp), room, n_shards))
    down_grad = down_layer(hw, cs)
    token_grad, route = home_rows(ids, halves, width, per_device, room, n_shards)
    return token_grad, route[:, :1], down_grad


def agreed(own_x, width, n_dp):
    flag = jnp.max(own_x[:, width + OVER : width + OVER + 1].astype(F32))
    flag = jnp.broadcast_to(flag, (8, 128))
    for step in range(1, lax.axis_size("groups")):
        flag = jnp.maximum(flag, shifted(flag, "groups", step))
    for bit in dp_bits(n_dp):
        flag = jnp.maximum(flag, swapped(flag, "dp", bit))
    return flag[0, 0]


def shards(tokens, out_grad, route_weight, expert_ids, gate, up, down):
    n_shards, n_dp = lax.axis_size("expert"), lax.axis_size("dp")
    per_device, width = gate.shape[0], tokens.shape[1]
    most_rows = min(expert_ids.shape[0], per_device * MOST)
    ids = expert_ids
    if direct(n_shards):
        total = n_shards * per_device
        ids = (ids - lax.axis_index("expert") * per_device + total) % total
    gate, up = jnp.swapaxes(gate, 1, 2), jnp.swapaxes(up, 1, 2)
    usual = most_rows * 5 // 8
    adaptive = direct(n_shards) and usual % 8 == 0 and (n_shards * usual) % 16 == 0
    room = usual if adaptive else most_rows
    own_x, own_c = begin(room, ids, tokens, out_grad, route_weight, per_device)
    x_list = gather_dp(own_x, n_dp)
    if not adaptive:
        return finish(room, ids, x_list, own_c, gate, up, down)
    over = agreed(own_x, width, n_dp)

    def fits(_):
        return finish(room, ids, x_list, own_c, gate, up, down)

    def full(_):
        full_x, full_c = begin(most_rows, ids, tokens, out_grad, route_weight, per_device)
        return finish(most_rows, ids, gather_dp(full_x, n_dp), full_c, gate, up, down)

    return lax.cond(over > 0.0, full, fits, 0)


def solution(mesh):
    rows = P(("groups", "expert", "dp"), None)
    in_specs = (
        rows,
        rows,
        rows,
        rows,
        P("expert", None, "dp"),
        P("expert", None, "dp"),
        P("expert", "dp", None),
    )
    out_specs = (rows, rows, P(("groups", "expert"), "dp", None))
    return jax.shard_map(shards, mesh=mesh, in_specs=in_specs, out_specs=out_specs, check_vma=False)
```

```python
import functools

import jax
import jax.numpy as jnp
from jax import lax
from jax.experimental import pallas as pl
from jax.experimental.pallas import tpu as pltpu
from jax.sharding import PartitionSpec as P

MOST = 4
META = 128
OVER = 2
BF = jnp.bfloat16
F32 = jnp.float32
VMEM_BYTES = 48 * 1024 * 1024


def dot_nn(a, b):
    return jnp.dot(a, b, preferred_element_type=F32)


def dot_nt(a, b):
    return lax.dot_general(a, b, (((1,), (1,)), ((), ())), preferred_element_type=F32)


def dot_tn(a, b):
    return lax.dot_general(a, b, (((0,), (0,)), ((), ())), preferred_element_type=F32)


def params():
    return pltpu.CompilerParams(vmem_limit_bytes=VMEM_BYTES)


def cost(flops, moved):
    return pl.CostEstimate(flops=int(flops), bytes_accessed=int(moved), transcendentals=0)


def step_of(experts, most):
    step = 1
    while step * 2 <= most and experts % (step * 2) == 0:
        step *= 2
    return step


def whole(array):
    zeros = (0,) * array.ndim
    return pl.BlockSpec(array.shape, lambda *_: zeros)


def route_columns(ids, per_device, n_shards):
    count = ids.shape[1]
    here = lax.axis_index("expert") if direct(n_shards) else 0
    total = n_shards * per_device
    ids = ids - here * per_device
    ids = jnp.where(ids < 0, ids + total, ids)
    down = jnp.broadcast_to(ids.astype(F32), (count, count))
    across = jnp.transpose(down)
    row = lax.broadcasted_iota(jnp.int32, (count, count), 0)
    col = lax.broadcasted_iota(jnp.int32, (count, count), 1)
    earlier = col < row
    inv = 1.0 / per_device
    across_shard = jnp.floor((across + 0.5) * inv)
    same_expert = jnp.where((across == down) & earlier, 1.0, 0.0)
    same_shard = jnp.where(
        (across_shard == jnp.floor((down + 0.5) * inv)) & earlier, 1.0, 0.0
    )
    rank = jnp.sum(same_expert, axis=1, keepdims=True)
    place = jnp.sum(same_shard, axis=1, keepdims=True)
    shard = across_shard[:, 0:1]
    local = across[:, 0:1] - shard * per_device
    return shard, local, rank, place


def slot_table(ids, per_device, room, n_shards):
    shard, local, rank, place = route_columns(ids, per_device, n_shards)
    slot = jnp.where(place < room, shard * room + place, -1.0).astype(jnp.int32)
    lanes = lax.broadcasted_iota(jnp.int32, (ids.shape[1], n_shards * room), 1)
    over = jnp.max(place, axis=0, keepdims=True) >= room
    return jnp.where(lanes == slot, 1.0, 0.0).astype(BF), local * MOST + rank + 1.0, over


def pack_kernel(per_device, room, n_shards, ids_ref, tok_ref, cot_ref, wgt_ref, x_ref, c_ref):
    table, tag, over = slot_table(ids_ref[...], per_device, room, n_shards)
    width = tok_ref.shape[1]
    x_ref[:, :width] = dot_tn(table, tok_ref[...]).astype(BF)
    lane = lax.broadcasted_iota(jnp.int32, (tag.shape[0], META), 1)
    count = tok_ref.shape[0]
    wgt = jnp.transpose(jnp.broadcast_to(wgt_ref[...].astype(F32), (count, count)))[:, 0:1]
    info = jnp.where(lane == 0, tag, jnp.where(lane == 1, wgt, 0.0))
    packed = dot_tn(table, info.astype(BF))
    lane = lax.broadcasted_iota(jnp.int32, packed.shape, 1)
    flag = jnp.broadcast_to(jnp.where(over, 1.0, 0.0), packed.shape)
    x_ref[:, width:] = jnp.where(lane == OVER, flag, packed).astype(BF)
    c_ref[...] = dot_tn(table, cot_ref[...]).astype(BF)


def pack_rows(ids, tokens, out_grad, wgt, per_device, room, n_shards):
    rows, width = n_shards * room, tokens.shape[1]
    args = (ids, tokens, out_grad, wgt)
    return pl.pallas_call(
        functools.partial(pack_kernel, per_device, room, n_shards),
        grid=(1,),
        in_specs=[whole(a) for a in args],
        out_specs=[
            pl.BlockSpec((rows, width + META), lambda i: (0, 0)),
            pl.BlockSpec((rows, width), lambda i: (0, 0)),
        ],
        out_shape=[
            jax.ShapeDtypeStruct((rows, width + META), BF),
            jax.ShapeDtypeStruct((rows, width), BF),
        ],
        compiler_params=params(),
        cost_estimate=cost(4e8, 4e6),
        name="pack_rows",
    )(*args)


def sorted_table(meta, room, n_shards, n_sorted):
    tag = meta[:, 0:1].astype(F32).astype(jnp.int32)
    rows = lax.broadcasted_iota(jnp.int32, tag.shape, 0)
    source = jnp.floor((rows.astype(F32) + 0.5) * (1.0 / room)).astype(jnp.int32)
    at = tag - 1
    local = at // MOST
    dest = local * (n_shards * MOST) + source * MOST + (at - local * MOST)
    dest = jnp.where(tag > 0, dest, -1)
    lanes = lax.broadcasted_iota(jnp.int32, (meta.shape[0], n_sorted), 1)
    return jnp.where(lanes == dest, 1.0, 0.0).astype(BF)


def spread(table, rows_ref, width, out_ref, member, chunk=512):
    experts, _, _ = out_ref.shape
    per_expert = table.shape[1] // experts
    turned = jnp.transpose(table)
    low = member * per_expert
    for c in range(0, width, chunk):
        part = dot_nn(turned, rows_ref[:, c : c + chunk]).astype(BF)
        out_ref[:, low : low + per_expert, c : c + chunk] = part.reshape(
            experts, per_expert, chunk
        )


def first_kernel(n_dp, room, n_shards, *refs):
    x_refs = refs[:n_dp]
    gate_ref, up_ref, g_ref, u_ref, xs = refs[n_dp:]
    experts, expert_rows, width = xs.shape
    n_sorted = experts * expert_rows // n_dp

    @pl.when(pl.program_id(0) == 0)
    def _():
        for d in range(n_dp):
            table = sorted_table(x_refs[d][:, width : width + META], room, n_shards, n_sorted)
            spread(table, x_refs[d], width, xs, d)

    step = gate_ref.shape[0]
    for i in range(step):
        x_block = xs[pl.program_id(0) * step + i]
        g_ref[i] = dot_nt(x_block, gate_ref[i])
        u_ref[i] = dot_nt(x_block, up_ref[i])


def first_layer(x_list, gate, up, room, n_shards):
    n_dp = len(x_list)
    experts, hidden, width = gate.shape
    expert_rows = n_dp * n_shards * MOST
    step = step_of(experts, 4)
    by_expert = lambda e: (e, 0, 0)
    shape = jax.ShapeDtypeStruct((experts, expert_rows, hidden), F32)
    return pl.pallas_call(
        functools.partial(first_kernel, n_dp, room, n_shards),
        grid=(experts // step,),
        in_specs=[whole(x) for x in x_list]
        + [pl.BlockSpec((step, hidden, width), by_expert)] * 2,
        out_specs=[pl.BlockSpec((step, expert_rows, hidden), by_expert)] * 2,
        out_shape=[shape, shape],
        scratch_shapes=[pltpu.VMEM((experts, expert_rows, width), BF)],
        compiler_params=params(),
        cost_estimate=cost(2e9, 3e7),
        name="gate_up",
    )(*x_list, gate, up)


def second_kernel(n_dp, room, n_shards, *refs):
    m_refs, c_refs = refs[:n_dp], refs[n_dp : 2 * n_dp]
    g_ref, u_ref, down_ref, dg_ref, du_ref, hw_ref, cs_ref, r_ref, cs, ms = refs[2 * n_dp :]
    experts, expert_rows, width = cs.shape
    n_sorted = experts * expert_rows // n_dp

    @pl.when(pl.program_id(0) == 0)
    def _():
        for d in range(n_dp):
            meta = m_refs[d][...]
            table = sorted_table(meta, room, n_shards, n_sorted)
            spread(table, c_refs[d], width, cs, d)
            spread(table, m_refs[d], META, ms, d, META)

    step = g_ref.shape[0]
    for i in range(step):
        at = pl.program_id(0) * step + i
        c_block = cs[at]
        cs_ref[i] = c_block
        weight = ms[at][:, 1:2].astype(F32)
        back = dot_nt(c_block, down_ref[i])
        g, u = g_ref[i], u_ref[i]
        sig = jax.nn.sigmoid(g)
        act = g * sig
        hidden = act * u
        router = jnp.sum(hidden.astype(BF).astype(F32) * back, axis=1, keepdims=True)
        r_ref[i] = jnp.broadcast_to(router, (expert_rows, META)).astype(BF)
        hw_ref[i] = (hidden * weight).astype(BF)
        scaled = back * weight
        dg_ref[i] = (scaled * u * (sig * (1.0 + g * (1.0 - sig)))).astype(BF)
        du_ref[i] = (scaled * act).astype(BF)


def second_layer(x_list, c_list, g, u, down, room, n_shards):
    n_dp = len(c_list)
    experts, hidden, width = down.shape
    expert_rows = g.shape[1]
    slots = c_list[0].shape[0]
    step = step_of(experts, 4)
    by_expert = lambda e: (e, 0, 0)
    small = jax.ShapeDtypeStruct((experts, expert_rows, hidden), BF)
    small_spec = pl.BlockSpec((step, expert_rows, hidden), by_expert)
    return pl.pallas_call(
        functools.partial(second_kernel, n_dp, room, n_shards),
        grid=(experts // step,),
        in_specs=[pl.BlockSpec((slots, META), lambda e: (0, width // META))] * n_dp
        + [whole(c) for c in c_list]
        + [small_spec] * 2
        + [pl.BlockSpec((step, hidden, width), by_expert)],
        out_specs=[small_spec] * 3
        + [
            pl.BlockSpec((step, expert_rows, width), by_expert),
            pl.BlockSpec((step, expert_rows, META), by_expert),
        ],
        out_shape=[small] * 3
        + [
            jax.ShapeDtypeStruct((experts, expert_rows, width), BF),
            jax.ShapeDtypeStruct((experts, expert_rows, META), BF),
        ],
        scratch_shapes=[
            pltpu.VMEM((experts, expert_rows, width), BF),
            pltpu.VMEM((experts, expert_rows, META), BF),
        ],
        compiler_params=params(),
        cost_estimate=cost(2e9, 2e7),
        name="hidden_grads",
    )(*x_list, *c_list, g, u, down)


def third_kernel(n_dp, room, n_shards, with_router, *refs):
    m_refs = refs[:n_dp]
    rest = refs[n_dp:]
    dg_ref, du_ref, gate_ref, up_ref = rest[:4]
    rest = rest[4:]
    if with_router:
        r_ref, rest = rest[0], rest[1:]
    out_refs, acc = rest[:n_dp], rest[n_dp]
    _, experts, per_expert, width = acc.shape
    step, _, part = gate_ref.shape
    for i in range(step):
        at = pl.program_id(0) * step + i
        grad = (dot_nn(dg_ref[i], gate_ref[i]) + dot_nn(du_ref[i], up_ref[i])).astype(BF)
        for d in range(n_dp):
            low = d * per_expert
            acc[d, at, :, :part] = grad[low : low + per_expert]
            if with_router:
                acc[d, at, :, part:] = r_ref[i, low : low + per_expert]

    @pl.when(pl.program_id(0) == pl.num_programs(0) - 1)
    def _():
        for d in range(n_dp):
            table = sorted_table(m_refs[d][...], room, n_shards, experts * per_expert)
            rows = acc[d].reshape(experts * per_expert, width)
            out_refs[d][...] = dot_nn(table, rows).astype(BF)


def third_layer(x_list, dg, du, gate, up, router, half, n_half, room, n_shards):
    n_dp = len(x_list)
    experts, hidden, full = gate.shape
    expert_rows = dg.shape[1]
    slots = x_list[0].shape[0]
    part = full // n_half
    width = part + (0 if router is None else META)
    step = step_of(experts, 4)
    by_expert = lambda e: (e, 0, 0)
    small_spec = pl.BlockSpec((step, expert_rows, hidden), by_expert)
    weight_spec = pl.BlockSpec((step, hidden, part), lambda e: (e, 0, half))
    args = [*x_list, dg, du, gate, up]
    specs = [pl.BlockSpec((slots, META), lambda e: (0, full // META))] * n_dp
    specs += [small_spec] * 2 + [weight_spec] * 2
    if router is not None:
        args.append(router)
        specs.append(pl.BlockSpec((step, expert_rows, META), by_expert))
    return pl.pallas_call(
        functools.partial(third_kernel, n_dp, room, n_shards, router is not None),
        grid=(experts // step,),
        in_specs=specs,
        out_specs=[pl.BlockSpec((slots, width), lambda e: (0, 0))] * n_dp,
        out_shape=[jax.ShapeDtypeStruct((slots, width), BF)] * n_dp,
        scratch_shapes=[pltpu.VMEM((n_dp, experts, expert_rows // n_dp, width), BF)],
        compiler_params=params(),
        cost_estimate=cost(1e9, 1.5e7),
        name="input_grads",
    )(*args)


def down_kernel(hw_ref, cs_ref, out_ref):
    for i in range(hw_ref.shape[0]):
        out_ref[i] = dot_tn(hw_ref[i], cs_ref[i]).astype(BF)


def down_layer(hw, cs):
    experts, rows, hidden = hw.shape
    width = cs.shape[2]
    step = step_of(experts, 4)
    by_expert = lambda e: (e, 0, 0)
    return pl.pallas_call(
        down_kernel,
        grid=(experts // step,),
        in_specs=[
            pl.BlockSpec((step, rows, hidden), by_expert),
            pl.BlockSpec((step, rows, width), by_expert),
        ],
        out_specs=pl.BlockSpec((step, hidden, width), by_expert),
        out_shape=jax.ShapeDtypeStruct((experts, hidden, width), BF),
        compiler_params=params(),
        cost_estimate=cost(1e9, 1.8e7),
        name="down_grads",
    )(hw, cs)


def home_kernel(per_device, room, n_shards, n_half, n_blocks, ids_ref, *refs):
    table, _, _ = slot_table(ids_ref[...], per_device, room, n_shards)
    blocks, (tok_ref, route_ref) = refs[:-2], refs[-2:]
    part = tok_ref.shape[1] // n_half
    size = n_shards * room // n_blocks
    for h in range(n_half):
        total = None
        for k in range(n_blocks):
            term = dot_nn(table[:, k * size : (k + 1) * size], blocks[h * n_blocks + k][...])
            total = term if total is None else total + term
        tok_ref[:, h * part : (h + 1) * part] = total[:, :part].astype(BF)
        if h == 0:
            column = jnp.broadcast_to(total[:, part : part + 1], (total.shape[0],) * 2)
            route_ref[...] = jnp.transpose(column)[0:1].astype(BF)


def home_rows(ids, halves, width, per_device, room, n_shards):
    n_half, n_blocks = len(halves), len(halves[0])
    count = ids.shape[1]
    blocks = [b for half in halves for b in half]
    return pl.pallas_call(
        functools.partial(home_kernel, per_device, room, n_shards, n_half, n_blocks),
        grid=(1,),
        in_specs=[whole(ids)] + [whole(b) for b in blocks],
        out_specs=[
            pl.BlockSpec((count, width), lambda i: (0, 0)),
            pl.BlockSpec((1, count), lambda i: (0, 0)),
        ],
        out_shape=[
            jax.ShapeDtypeStruct((count, width), BF),
            jax.ShapeDtypeStruct((1, count), BF),
        ],
        compiler_params=params(),
        cost_estimate=cost(2e8, 2e6),
        name="home_rows",
    )(ids, *blocks)


def shifted(value, axis, step):
    n = lax.axis_size(axis)
    return lax.ppermute(value, axis, [(i, (i + step) % n) for i in range(n)])


def swapped(value, axis, bit):
    n = lax.axis_size(axis)
    return lax.ppermute(value, axis, [(i, i ^ bit) for i in range(n)])


def after(value, other):
    return lax.optimization_barrier((value, other))[0]


def direct(n_shards):
    return n_shards <= 4


def to_shards(rows, room, n_shards):
    return join_shards(shard_parts(rows, room, n_shards))


def shard_parts(rows, room, n_shards):
    if not direct(n_shards):
        shaped = rows.reshape(n_shards, room, rows.shape[1])
        return [lax.all_to_all(shaped, "expert", 0, 0, tiled=True).reshape(rows.shape)]
    parts = [rows[:room]]
    for k in range(1, n_shards):
        parts.append(shifted(rows[k * room : (k + 1) * room], "expert", k))
    return parts


def join_shards(parts):
    return parts[0] if len(parts) == 1 else jnp.concatenate(parts)


def from_shards(rows, room, n_shards):
    if not direct(n_shards):
        return [to_shards(rows, room, n_shards)]
    parts = [rows[:room]]
    for k in range(1, n_shards):
        parts.append(shifted(rows[k * room : (k + 1) * room], "expert", -k))
    return parts


def dp_bits(n_dp):
    bits, bit = [], 1
    while bit < n_dp:
        bits.append(bit)
        bit *= 2
    return bits


def far_hop(rows, n_dp):
    return swapped(rows, "dp", dp_bits(n_dp)[-1])


def near_hops(rows, n_dp):
    got = [rows]
    for bit in dp_bits(n_dp)[:-1]:
        got = got + [swapped(r, "dp", bit) for r in got]
    return got


def add_rows(a, b):
    return (a.astype(F32) + b.astype(F32)).astype(BF)


def near_sums(parts, n_dp):
    have = dict(enumerate(parts))
    for bit in dp_bits(n_dp)[:-1]:
        left = {}
        for k in sorted(have, reverse=True):
            if k & bit == 0:
                left[k] = add_rows(have[k], swapped(have[k ^ bit], "dp", bit))
        have = left
    return have[0], have[dp_bits(n_dp)[-1]]


def finish(room, ids, near_x, far_x, own_c, gate, up, down):
    n_shards, n_dp = lax.axis_size("expert"), lax.axis_size("dp")
    per_device, width = gate.shape[0], down.shape[2]
    far_c = far_hop(own_c, n_dp)
    x_list = near_x + near_hops(far_x, n_dp)
    g, u = first_layer(x_list, gate, up, room, n_shards)
    c_list = near_hops(own_c, n_dp) + near_hops(after(far_c, g), n_dp)
    dg, du, hw, cs, router = second_layer(x_list, c_list, g, u, down, room, n_shards)
    first = third_layer(x_list, dg, du, gate, up, router, 0, 2, room, n_shards)
    stay_1, go_1 = near_sums(first, n_dp)
    come_1 = far_hop(go_1, n_dp)
    dg, du = lax.optimization_barrier((dg, du, go_1))[:2]
    second = third_layer(x_list, dg, du, gate, up, None, 1, 2, room, n_shards)
    second = after(second, come_1)
    stay_2, go_2 = near_sums(second, n_dp)
    come_2 = far_hop(go_2, n_dp)
    down_grad = down_layer(after(hw, go_2), cs)
    home_1 = from_shards(add_rows(stay_1, come_1), room, n_shards)
    come_2 = after(come_2, (down_grad, home_1))
    home_2 = from_shards(add_rows(stay_2, come_2), room, n_shards)
    token_grad, route = home_rows(ids, [home_1, home_2], width, per_device, room, n_shards)
    return token_grad, route.reshape(-1, 1), down_grad


def exchange(room, ids, tokens, out_grad, route_weight, per_device, n_shards, n_dp):
    send_x, send_c = pack_rows(ids, tokens, out_grad, route_weight, per_device, room, n_shards)
    own_x = join_shards(shard_parts(send_x, room, n_shards))
    send_c, own_x = lax.optimization_barrier((send_c, own_x))
    far_x, near_x = far_hop(own_x, n_dp), near_hops(own_x, n_dp)
    return near_x, far_x, shard_parts(send_c, room, n_shards)


def agreed(flag, n_dp):
    for step in range(1, lax.axis_size("groups")):
        flag = jnp.maximum(flag, shifted(flag, "groups", step))
    for bit in dp_bits(n_dp):
        flag = jnp.maximum(flag, swapped(flag, "dp", bit))
    return flag


def shards(tokens, out_grad, route_weight, expert_ids, gate, up, down):
    n_shards, n_dp = lax.axis_size("expert"), lax.axis_size("dp")
    per_device, width = gate.shape[0], tokens.shape[1]
    most_rows = min(expert_ids.shape[0], per_device * MOST)
    ids, route_weight = expert_ids.reshape(1, -1), route_weight.reshape(1, -1)
    gate, up = jnp.swapaxes(gate, 1, 2), jnp.swapaxes(up, 1, 2)
    usual = most_rows * 5 // 8
    adaptive = direct(n_shards) and usual % 8 == 0 and (n_shards * usual) % 16 == 0
    room = usual if adaptive else most_rows
    args = (ids, tokens, out_grad, route_weight, per_device, n_shards, n_dp)
    near_x, far_x, parts_c = exchange(room, *args)
    if not adaptive:
        return finish(room, ids, near_x, far_x, join_shards(parts_c), gate, up, down)
    meta = near_x[0][:, width : width + META].astype(F32)
    over = jnp.max(meta, axis=0, keepdims=True)
    over = agreed(after(jnp.broadcast_to(over, (8, META)), near_x[-1]), n_dp)
    own_c = join_shards(parts_c)
    far_x, own_c, over = lax.optimization_barrier((far_x, own_c, over))

    def fits(_):
        return finish(room, ids, near_x, far_x, own_c, gate, up, down)

    def full(_):
        full_near, full_far, full_c = exchange(most_rows, *args)
        return finish(most_rows, ids, full_near, full_far, join_shards(full_c), gate, up, down)

    return lax.cond(over[0, OVER] > 0.0, full, fits, 0)


def solution(mesh):
    rows = P(("groups", "expert", "dp"), None)
    in_specs = (
        rows,
        rows,
        rows,
        rows,
        P("expert", None, "dp"),
        P("expert", None, "dp"),
        P("expert", "dp", None),
    )
    out_specs = (rows, rows, P(("groups", "expert"), "dp", None))
    return jax.shard_map(shards, mesh=mesh, in_specs=in_specs, out_specs=out_specs, check_vma=False)
```

```python
import functools

import jax
import jax.numpy as jnp
from jax import lax
from jax.experimental import pallas as pl
from jax.experimental.pallas import tpu as pltpu
from jax.sharding import PartitionSpec as P

MOST = 4
META = 128
OVER = 2
BF = jnp.bfloat16
F32 = jnp.float32
MIB = 1024 * 1024


def dot_nn(a, b):
    return jnp.dot(a, b, preferred_element_type=F32)


def dot_nt(a, b):
    return lax.dot_general(a, b, (((1,), (1,)), ((), ())), preferred_element_type=F32)


def dot_tn(a, b):
    return lax.dot_general(a, b, (((0,), (0,)), ((), ())), preferred_element_type=F32)


def params(mib=18):
    return pltpu.CompilerParams(vmem_limit_bytes=mib * MIB)


def big_limit(rows):
    return 20 + -(-8 * rows.shape[0] * rows.shape[1] * 2 // MIB)


def cost(flops, moved):
    return pl.CostEstimate(flops=int(flops), bytes_accessed=int(moved), transcendentals=0)


def step_of(experts, most):
    step = 1
    while step * 2 <= most and experts % (step * 2) == 0:
        step *= 2
    return step


def whole(array):
    zeros = (0,) * array.ndim
    return pl.BlockSpec(array.shape, lambda *_: zeros)


def route_columns(ids, per_device, n_shards):
    count = ids.shape[1]
    here = lax.axis_index("expert") if direct(n_shards) else 0
    total = n_shards * per_device
    ids = ids - here * per_device
    ids = jnp.where(ids < 0, ids + total, ids)
    down = jnp.broadcast_to(ids.astype(F32), (count, count))
    across = jnp.transpose(down)
    row = lax.broadcasted_iota(jnp.int32, (count, count), 0)
    col = lax.broadcasted_iota(jnp.int32, (count, count), 1)
    earlier = col < row
    inv = 1.0 / per_device
    across_shard = jnp.floor((across + 0.5) * inv)
    same_expert = jnp.where((across == down) & earlier, 1.0, 0.0)
    same_shard = jnp.where(
        (across_shard == jnp.floor((down + 0.5) * inv)) & earlier, 1.0, 0.0
    )
    rank = jnp.sum(same_expert, axis=1, keepdims=True)
    place = jnp.sum(same_shard, axis=1, keepdims=True)
    shard = across_shard[:, 0:1]
    local = across[:, 0:1] - shard * per_device
    return shard, local, rank, place


def slot_table(ids, per_device, room, n_shards):
    shard, local, rank, place = route_columns(ids, per_device, n_shards)
    slot = jnp.where(place < room, shard * room + place, -1.0).astype(jnp.int32)
    lanes = lax.broadcasted_iota(jnp.int32, (ids.shape[1], n_shards * room), 1)
    over = jnp.max(place, axis=0, keepdims=True) >= room
    return jnp.where(lanes == slot, 1.0, 0.0).astype(BF), local * MOST + rank + 1.0, over


def pack_kernel(per_device, room, n_shards, ids_ref, tok_ref, cot_ref, wgt_ref, x_ref, c_ref):
    table, tag, over = slot_table(ids_ref[...], per_device, room, n_shards)
    width = tok_ref.shape[1]
    x_ref[:, :width] = dot_tn(table, tok_ref[...]).astype(BF)
    lane = lax.broadcasted_iota(jnp.int32, (tag.shape[0], META), 1)
    count = tok_ref.shape[0]
    wgt = jnp.transpose(jnp.broadcast_to(wgt_ref[...].astype(F32), (count, count)))[:, 0:1]
    info = jnp.where(lane == 0, tag, jnp.where(lane == 1, wgt, 0.0))
    packed = dot_tn(table, info.astype(BF))
    lane = lax.broadcasted_iota(jnp.int32, packed.shape, 1)
    flag = jnp.broadcast_to(jnp.where(over, 1.0, 0.0), packed.shape)
    x_ref[:, width:] = jnp.where(lane == OVER, flag, packed).astype(BF)
    c_ref[...] = dot_tn(table, cot_ref[...]).astype(BF)


def pack_rows(ids, tokens, out_grad, wgt, per_device, room, n_shards):
    rows, width = n_shards * room, tokens.shape[1]
    args = (ids, tokens, out_grad, wgt)
    return pl.pallas_call(
        functools.partial(pack_kernel, per_device, room, n_shards),
        grid=(1,),
        in_specs=[whole(a) for a in args],
        out_specs=[
            pl.BlockSpec((rows, width + META), lambda i: (0, 0)),
            pl.BlockSpec((rows, width), lambda i: (0, 0)),
        ],
        out_shape=[
            jax.ShapeDtypeStruct((rows, width + META), BF),
            jax.ShapeDtypeStruct((rows, width), BF),
        ],
        compiler_params=params(),
        cost_estimate=cost(4e8, 4e6),
        name="pack_rows",
    )(*args)


def sorted_table(meta, room, n_shards, n_sorted):
    tag = meta[:, 0:1].astype(F32).astype(jnp.int32)
    rows = lax.broadcasted_iota(jnp.int32, tag.shape, 0)
    source = jnp.floor((rows.astype(F32) + 0.5) * (1.0 / room)).astype(jnp.int32)
    at = tag - 1
    local = at // MOST
    dest = local * (n_shards * MOST) + source * MOST + (at - local * MOST)
    dest = jnp.where(tag > 0, dest, -1)
    lanes = lax.broadcasted_iota(jnp.int32, (meta.shape[0], n_sorted), 1)
    return jnp.where(lanes == dest, 1.0, 0.0).astype(BF)


def spread(table, rows_ref, width, out_ref, member, chunk=512):
    experts, _, _ = out_ref.shape
    per_expert = table.shape[1] // experts
    turned = jnp.transpose(table)
    low = member * per_expert
    for c in range(0, width, chunk):
        part = dot_nn(turned, rows_ref[:, c : c + chunk]).astype(BF)
        out_ref[:, low : low + per_expert, c : c + chunk] = part.reshape(
            experts, per_expert, chunk
        )


def first_kernel(n_dp, room, n_shards, *refs):
    x_refs = refs[:n_dp]
    gate_ref, up_ref, g_ref, u_ref, xs = refs[n_dp:]
    experts, expert_rows, width = xs.shape
    n_sorted = experts * expert_rows // n_dp

    @pl.when(pl.program_id(0) == 0)
    def _():
        for d in range(n_dp):
            table = sorted_table(x_refs[d][:, width : width + META], room, n_shards, n_sorted)
            spread(table, x_refs[d], width, xs, d)

    step = gate_ref.shape[0]
    for i in range(step):
        x_block = xs[pl.program_id(0) * step + i]
        g_ref[i] = dot_nt(x_block, gate_ref[i])
        u_ref[i] = dot_nt(x_block, up_ref[i])


def first_layer(x_list, gate, up, room, n_shards):
    n_dp = len(x_list)
    experts, hidden, width = gate.shape
    expert_rows = n_dp * n_shards * MOST
    step = step_of(experts, 4)
    by_expert = lambda e: (e, 0, 0)
    shape = jax.ShapeDtypeStruct((experts, expert_rows, hidden), F32)
    return pl.pallas_call(
        functools.partial(first_kernel, n_dp, room, n_shards),
        grid=(experts // step,),
        in_specs=[whole(x) for x in x_list]
        + [pl.BlockSpec((step, hidden, width), by_expert)] * 2,
        out_specs=[pl.BlockSpec((step, expert_rows, hidden), by_expert)] * 2,
        out_shape=[shape, shape],
        scratch_shapes=[pltpu.VMEM((experts, expert_rows, width), BF)],
        compiler_params=params(big_limit(x_list[0])),
        cost_estimate=cost(2e9, 3e7),
        name="gate_up",
    )(*x_list, gate, up)


def second_kernel(n_dp, room, n_shards, *refs):
    m_refs, c_refs = refs[:n_dp], refs[n_dp : 2 * n_dp]
    g_ref, u_ref, down_ref, dg_ref, du_ref, hw_ref, cs_ref, r_ref, cs, ms = refs[2 * n_dp :]
    experts, expert_rows, width = cs.shape
    n_sorted = experts * expert_rows // n_dp

    @pl.when(pl.program_id(0) == 0)
    def _():
        for d in range(n_dp):
            meta = m_refs[d][...]
            table = sorted_table(meta, room, n_shards, n_sorted)
            spread(table, c_refs[d], width, cs, d)
            spread(table, m_refs[d], META, ms, d, META)

    step = g_ref.shape[0]
    for i in range(step):
        at = pl.program_id(0) * step + i
        c_block = cs[at]
        cs_ref[i] = c_block
        weight = ms[at][:, 1:2].astype(F32)
        back = dot_nt(c_block, down_ref[i])
        g, u = g_ref[i], u_ref[i]
        sig = jax.nn.sigmoid(g)
        act = g * sig
        hidden = act * u
        router = jnp.sum(hidden.astype(BF).astype(F32) * back, axis=1, keepdims=True)
        r_ref[i] = jnp.broadcast_to(router, (expert_rows, META)).astype(BF)
        hw_ref[i] = (hidden * weight).astype(BF)
        scaled = back * weight
        dg_ref[i] = (scaled * u * (sig * (1.0 + g * (1.0 - sig)))).astype(BF)
        du_ref[i] = (scaled * act).astype(BF)


def second_layer(x_list, c_list, g, u, down, room, n_shards):
    n_dp = len(c_list)
    experts, hidden, width = down.shape
    expert_rows = g.shape[1]
    slots = c_list[0].shape[0]
    step = step_of(experts, 4)
    by_expert = lambda e: (e, 0, 0)
    small = jax.ShapeDtypeStruct((experts, expert_rows, hidden), BF)
    small_spec = pl.BlockSpec((step, expert_rows, hidden), by_expert)
    return pl.pallas_call(
        functools.partial(second_kernel, n_dp, room, n_shards),
        grid=(experts // step,),
        in_specs=[pl.BlockSpec((slots, META), lambda e: (0, width // META))] * n_dp
        + [whole(c) for c in c_list]
        + [small_spec] * 2
        + [pl.BlockSpec((step, hidden, width), by_expert)],
        out_specs=[small_spec] * 3
        + [
            pl.BlockSpec((step, expert_rows, width), by_expert),
            pl.BlockSpec((step, expert_rows, META), by_expert),
        ],
        out_shape=[small] * 3
        + [
            jax.ShapeDtypeStruct((experts, expert_rows, width), BF),
            jax.ShapeDtypeStruct((experts, expert_rows, META), BF),
        ],
        scratch_shapes=[
            pltpu.VMEM((experts, expert_rows, width), BF),
            pltpu.VMEM((experts, expert_rows, META), BF),
        ],
        compiler_params=params(big_limit(c_list[0])),
        cost_estimate=cost(2e9, 2e7),
        name="hidden_grads",
    )(*x_list, *c_list, g, u, down)


def third_kernel(n_dp, room, n_shards, with_router, *refs):
    m_refs = refs[:n_dp]
    rest = refs[n_dp:]
    dg_ref, du_ref, gate_ref, up_ref = rest[:4]
    rest = rest[4:]
    if with_router:
        r_ref, rest = rest[0], rest[1:]
    out_refs, acc = rest[:n_dp], rest[n_dp]
    _, experts, per_expert, width = acc.shape
    step, _, part = gate_ref.shape
    for i in range(step):
        at = pl.program_id(0) * step + i
        grad = (dot_nn(dg_ref[i], gate_ref[i]) + dot_nn(du_ref[i], up_ref[i])).astype(BF)
        for d in range(n_dp):
            low = d * per_expert
            acc[d, at, :, :part] = grad[low : low + per_expert]
            if with_router:
                acc[d, at, :, part:] = r_ref[i, low : low + per_expert]

    @pl.when(pl.program_id(0) == pl.num_programs(0) - 1)
    def _():
        for d in range(n_dp):
            table = sorted_table(m_refs[d][...], room, n_shards, experts * per_expert)
            rows = acc[d].reshape(experts * per_expert, width)
            out_refs[d][...] = dot_nn(table, rows).astype(BF)


def third_layer(x_list, dg, du, gate, up, router, half, n_half, room, n_shards):
    n_dp = len(x_list)
    experts, hidden, full = gate.shape
    expert_rows = dg.shape[1]
    slots = x_list[0].shape[0]
    part = full // n_half
    width = part + (0 if router is None else META)
    step = step_of(experts, 4)
    by_expert = lambda e: (e, 0, 0)
    small_spec = pl.BlockSpec((step, expert_rows, hidden), by_expert)
    weight_spec = pl.BlockSpec((step, hidden, part), lambda e: (e, 0, half))
    args = [*x_list, dg, du, gate, up]
    specs = [pl.BlockSpec((slots, META), lambda e: (0, full // META))] * n_dp
    specs += [small_spec] * 2 + [weight_spec] * 2
    if router is not None:
        args.append(router)
        specs.append(pl.BlockSpec((step, expert_rows, META), by_expert))
    return pl.pallas_call(
        functools.partial(third_kernel, n_dp, room, n_shards, router is not None),
        grid=(experts // step,),
        in_specs=specs,
        out_specs=[pl.BlockSpec((slots, width), lambda e: (0, 0))] * n_dp,
        out_shape=[jax.ShapeDtypeStruct((slots, width), BF)] * n_dp,
        scratch_shapes=[pltpu.VMEM((n_dp, experts, expert_rows // n_dp, width), BF)],
        compiler_params=params(),
        cost_estimate=cost(1e9, 1.5e7),
        name="input_grads",
    )(*args)


def down_kernel(*refs):
    hw_ref, cs_ref, out_ref = refs[0], refs[1], refs[-1]
    for i in range(hw_ref.shape[0]):
        out_ref[i] = dot_tn(hw_ref[i], cs_ref[i]).astype(BF)


def down_layer(hw, cs, low, count, sofar=None):
    experts, rows, hidden = hw.shape
    width = cs.shape[2]
    step = step_of(count, 4)
    by_expert = lambda e: (e + low // step, 0, 0)
    more = [] if sofar is None else [sofar]
    return pl.pallas_call(
        down_kernel,
        grid=(count // step,),
        in_specs=[
            pl.BlockSpec((step, rows, hidden), by_expert),
            pl.BlockSpec((step, rows, width), by_expert),
        ]
        + [pl.BlockSpec(memory_space=pl.ANY)] * len(more),
        out_specs=pl.BlockSpec((step, hidden, width), by_expert),
        out_shape=jax.ShapeDtypeStruct((experts, hidden, width), BF),
        input_output_aliases={2: 0} if more else {},
        compiler_params=params(),
        cost_estimate=cost(5e8, 9e6),
        name="down_grads",
    )(hw, cs, *more)


def home_kernel(per_device, room, n_shards, n_half, n_blocks, ids_ref, *refs):
    table, _, _ = slot_table(ids_ref[...], per_device, room, n_shards)
    blocks, (tok_ref, route_ref) = refs[:-2], refs[-2:]
    part = tok_ref.shape[1] // n_half
    size = n_shards * room // n_blocks
    for h in range(n_half):
        total = None
        for k in range(n_blocks):
            term = dot_nn(table[:, k * size : (k + 1) * size], blocks[h * n_blocks + k][...])
            total = term if total is None else total + term
        tok_ref[:, h * part : (h + 1) * part] = total[:, :part].astype(BF)
        if h == 0:
            column = jnp.broadcast_to(total[:, part : part + 1], (total.shape[0],) * 2)
            route_ref[...] = jnp.transpose(column)[0:1].astype(BF)


def home_rows(ids, halves, width, per_device, room, n_shards):
    n_half, n_blocks = len(halves), len(halves[0])
    count = ids.shape[1]
    blocks = [b for half in halves for b in half]
    return pl.pallas_call(
        functools.partial(home_kernel, per_device, room, n_shards, n_half, n_blocks),
        grid=(1,),
        in_specs=[whole(ids)] + [whole(b) for b in blocks],
        out_specs=[
            pl.BlockSpec((count, width), lambda i: (0, 0)),
            pl.BlockSpec((1, count), lambda i: (0, 0)),
        ],
        out_shape=[
            jax.ShapeDtypeStruct((count, width), BF),
            jax.ShapeDtypeStruct((1, count), BF),
        ],
        compiler_params=params(),
        cost_estimate=cost(2e8, 2e6),
        name="home_rows",
    )(ids, *blocks)


def shifted(value, axis, step):
    n = lax.axis_size(axis)
    return lax.ppermute(value, axis, [(i, (i + step) % n) for i in range(n)])


def swapped(value, axis, bit):
    n = lax.axis_size(axis)
    return lax.ppermute(value, axis, [(i, i ^ bit) for i in range(n)])


def after(value, other):
    return lax.optimization_barrier((value, other))[0]


def direct(n_shards):
    return n_shards <= 4


def to_shards(rows, room, n_shards):
    return join_shards(shard_parts(rows, room, n_shards))


def shard_parts(rows, room, n_shards):
    if not direct(n_shards):
        shaped = rows.reshape(n_shards, room, rows.shape[1])
        return [lax.all_to_all(shaped, "expert", 0, 0, tiled=True).reshape(rows.shape)]
    parts = [rows[:room]]
    for k in range(1, n_shards):
        parts.append(shifted(rows[k * room : (k + 1) * room], "expert", k))
    return parts


def join_shards(parts):
    return parts[0] if len(parts) == 1 else jnp.concatenate(parts)


def from_shards(rows, room, n_shards):
    if not direct(n_shards):
        return [to_shards(rows, room, n_shards)]
    parts = [rows[:room]]
    for k in range(1, n_shards):
        parts.append(shifted(rows[k * room : (k + 1) * room], "expert", -k))
    return parts


def dp_bits(n_dp):
    bits, bit = [], 1
    while bit < n_dp:
        bits.append(bit)
        bit *= 2
    return bits


def far_hop(rows, n_dp):
    return swapped(rows, "dp", dp_bits(n_dp)[-1])


def near_hops(rows, n_dp):
    got = [rows]
    for bit in dp_bits(n_dp)[:-1]:
        got = got + [swapped(r, "dp", bit) for r in got]
    return got


def add_rows(a, b):
    return (a.astype(F32) + b.astype(F32)).astype(BF)


def near_sums(parts, n_dp):
    have = dict(enumerate(parts))
    for bit in dp_bits(n_dp)[:-1]:
        left = {}
        for k in sorted(have, reverse=True):
            if k & bit == 0:
                left[k] = add_rows(have[k], swapped(have[k ^ bit], "dp", bit))
        have = left
    return have[0], have[dp_bits(n_dp)[-1]]


def finish(room, ids, near_x, far_x, own_c, gate, up, down):
    n_shards, n_dp = lax.axis_size("expert"), lax.axis_size("dp")
    per_device, width = gate.shape[0], down.shape[2]
    far_c = far_hop(own_c, n_dp)
    x_list = near_x + near_hops(far_x, n_dp)
    g, u = first_layer(x_list, gate, up, room, n_shards)
    c_list = near_hops(own_c, n_dp) + near_hops(after(far_c, g), n_dp)
    dg, du, hw, cs, router = second_layer(x_list, c_list, g, u, down, room, n_shards)
    first = third_layer(x_list, dg, du, gate, up, router, 0, 2, room, n_shards)
    stay_1, go_1 = near_sums(first, n_dp)
    come_1 = far_hop(go_1, n_dp)
    dg, du = lax.optimization_barrier((dg, du, go_1))[:2]
    second = third_layer(x_list, dg, du, gate, up, None, 1, 2, room, n_shards)
    early = per_device // 2
    down_grad = down_layer(after(hw, second), cs, 0, early) if early else None
    second = after(second, (come_1, down_grad))
    stay_2, go_2 = near_sums(second, n_dp)
    come_2 = far_hop(go_2, n_dp)
    home_1 = from_shards(add_rows(stay_1, come_1), room, n_shards)
    down_grad = down_layer(after(hw, go_2), cs, early, per_device - early, down_grad)
    rows_2 = add_rows(stay_2, after(come_2, down_grad))
    home_2 = from_shards(rows_2, room, n_shards)
    token_grad, route = home_rows(ids, [home_1, home_2], width, per_device, room, n_shards)
    return token_grad, route.reshape(-1, 1), down_grad


def exchange(room, ids, tokens, out_grad, route_weight, per_device, n_shards, n_dp):
    send_x, send_c = pack_rows(ids, tokens, out_grad, route_weight, per_device, room, n_shards)
    own_x = join_shards(shard_parts(send_x, room, n_shards))
    send_c, own_x = lax.optimization_barrier((send_c, own_x))
    far_x, near_x = far_hop(own_x, n_dp), near_hops(own_x, n_dp)
    return near_x, far_x, shard_parts(send_c, room, n_shards)


def agreed(flag, n_dp):
    for step in range(1, lax.axis_size("groups")):
        flag = jnp.maximum(flag, shifted(flag, "groups", step))
    for bit in dp_bits(n_dp):
        flag = jnp.maximum(flag, swapped(flag, "dp", bit))
    return flag


def shards(tokens, out_grad, route_weight, expert_ids, gate, up, down):
    n_shards, n_dp = lax.axis_size("expert"), lax.axis_size("dp")
    per_device, width = gate.shape[0], tokens.shape[1]
    most_rows = min(expert_ids.shape[0], per_device * MOST)
    ids, route_weight = expert_ids.reshape(1, -1), route_weight.reshape(1, -1)
    gate, up = jnp.swapaxes(gate, 1, 2), jnp.swapaxes(up, 1, 2)
    usual = most_rows * 5 // 8
    adaptive = direct(n_shards) and usual % 8 == 0 and (n_shards * usual) % 16 == 0
    room = usual if adaptive else most_rows
    args = (ids, tokens, out_grad, route_weight, per_device, n_shards, n_dp)
    near_x, far_x, parts_c = exchange(room, *args)
    if not adaptive:
        return finish(room, ids, near_x, far_x, join_shards(parts_c), gate, up, down)
    meta = near_x[0][:, width : width + META].astype(F32)
    over = jnp.max(meta, axis=0, keepdims=True)
    over = agreed(after(jnp.broadcast_to(over, (8, META)), near_x[-1]), n_dp)
    own_c = join_shards(parts_c)
    far_x, own_c, over = lax.optimization_barrier((far_x, own_c, over))

    def fits(_):
        return finish(room, ids, near_x, far_x, own_c, gate, up, down)

    def full(_):
        full_near, full_far, full_c = exchange(most_rows, *args)
        return finish(most_rows, ids, full_near, full_far, join_shards(full_c), gate, up, down)

    return lax.cond(over[0, OVER] > 0.0, full, fits, 0)


def solution(mesh):
    rows = P(("groups", "expert", "dp"), None)
    in_specs = (
        rows,
        rows,
        rows,
        rows,
        P("expert", None, "dp"),
        P("expert", None, "dp"),
        P("expert", "dp", None),
    )
    out_specs = (rows, rows, P(("groups", "expert"), "dp", None))
    return jax.shard_map(shards, mesh=mesh, in_specs=in_specs, out_specs=out_specs, check_vma=False)
```

```python
import functools

import jax
import jax.numpy as jnp
from jax import lax
from jax.experimental import pallas as pl
from jax.experimental.pallas import tpu as pltpu
from jax.sharding import PartitionSpec as P

MOST = 4
META = 128
OVER = 2
BF = jnp.bfloat16
F32 = jnp.float32
MIB = 1024 * 1024


def dot_nn(a, b):
    return jnp.dot(a, b, preferred_element_type=F32)


def dot_nt(a, b):
    return lax.dot_general(a, b, (((1,), (1,)), ((), ())), preferred_element_type=F32)


def dot_tn(a, b):
    return lax.dot_general(a, b, (((0,), (0,)), ((), ())), preferred_element_type=F32)


def params(mib=18):
    return pltpu.CompilerParams(vmem_limit_bytes=mib * MIB)


def big_limit(rows):
    return 20 + -(-8 * rows.shape[0] * rows.shape[1] * 2 // MIB)


def cost(flops, moved):
    return pl.CostEstimate(flops=int(flops), bytes_accessed=int(moved), transcendentals=0)


def step_of(experts, most):
    step = 1
    while step * 2 <= most and experts % (step * 2) == 0:
        step *= 2
    return step


def whole(array):
    zeros = (0,) * array.ndim
    return pl.BlockSpec(array.shape, lambda *_: zeros)


def route_columns(ids, per_device, n_shards):
    count = ids.shape[1]
    here = lax.axis_index("expert") if direct(n_shards) else 0
    total = n_shards * per_device
    ids = ids - here * per_device
    ids = jnp.where(ids < 0, ids + total, ids)
    down = jnp.broadcast_to(ids.astype(F32), (count, count))
    across = jnp.transpose(down)
    row = lax.broadcasted_iota(jnp.int32, (count, count), 0)
    col = lax.broadcasted_iota(jnp.int32, (count, count), 1)
    earlier = col < row
    inv = 1.0 / per_device
    across_shard = jnp.floor((across + 0.5) * inv)
    same_expert = jnp.where((across == down) & earlier, 1.0, 0.0)
    same_shard = jnp.where(
        (across_shard == jnp.floor((down + 0.5) * inv)) & earlier, 1.0, 0.0
    )
    rank = jnp.sum(same_expert, axis=1, keepdims=True)
    place = jnp.sum(same_shard, axis=1, keepdims=True)
    shard = across_shard[:, 0:1]
    local = across[:, 0:1] - shard * per_device
    return shard, local, rank, place


def slot_table(ids, per_device, room, n_shards):
    shard, local, rank, place = route_columns(ids, per_device, n_shards)
    slot = jnp.where(place < room, shard * room + place, -1.0).astype(jnp.int32)
    lanes = lax.broadcasted_iota(jnp.int32, (ids.shape[1], n_shards * room), 1)
    over = jnp.max(place, axis=0, keepdims=True) >= room
    return jnp.where(lanes == slot, 1.0, 0.0).astype(BF), local * MOST + rank + 1.0, over


def pack_kernel(per_device, room, n_shards, ids_ref, tok_ref, cot_ref, wgt_ref, x_ref, c_ref):
    table, tag, over = slot_table(ids_ref[...], per_device, room, n_shards)
    width = tok_ref.shape[1]
    x_ref[:, :width] = dot_tn(table, tok_ref[...]).astype(BF)
    lane = lax.broadcasted_iota(jnp.int32, (tag.shape[0], META), 1)
    count = tok_ref.shape[0]
    wgt = jnp.transpose(jnp.broadcast_to(wgt_ref[...].astype(F32), (count, count)))[:, 0:1]
    info = jnp.where(lane == 0, tag, jnp.where(lane == 1, wgt, 0.0))
    packed = dot_tn(table, info.astype(BF))
    lane = lax.broadcasted_iota(jnp.int32, packed.shape, 1)
    flag = jnp.broadcast_to(jnp.where(over, 1.0, 0.0), packed.shape)
    x_ref[:, width:] = jnp.where(lane == OVER, flag, packed).astype(BF)
    c_ref[...] = dot_tn(table, cot_ref[...]).astype(BF)


def pack_rows(ids, tokens, out_grad, wgt, per_device, room, n_shards):
    rows, width = n_shards * room, tokens.shape[1]
    args = (ids, tokens, out_grad, wgt)
    return pl.pallas_call(
        functools.partial(pack_kernel, per_device, room, n_shards),
        grid=(1,),
        in_specs=[whole(a) for a in args],
        out_specs=[
            pl.BlockSpec((rows, width + META), lambda i: (0, 0)),
            pl.BlockSpec((rows, width), lambda i: (0, 0)),
        ],
        out_shape=[
            jax.ShapeDtypeStruct((rows, width + META), BF),
            jax.ShapeDtypeStruct((rows, width), BF),
        ],
        compiler_params=params(),
        cost_estimate=cost(4e8, 4e6),
        name="pack_rows",
    )(*args)


def sorted_table(meta, room, n_shards, n_sorted):
    tag = meta[:, 0:1].astype(F32).astype(jnp.int32)
    rows = lax.broadcasted_iota(jnp.int32, tag.shape, 0)
    source = jnp.floor((rows.astype(F32) + 0.5) * (1.0 / room)).astype(jnp.int32)
    at = tag - 1
    local = at // MOST
    dest = local * (n_shards * MOST) + source * MOST + (at - local * MOST)
    dest = jnp.where(tag > 0, dest, -1)
    lanes = lax.broadcasted_iota(jnp.int32, (meta.shape[0], n_sorted), 1)
    return jnp.where(lanes == dest, 1.0, 0.0).astype(BF)


def spread(table, rows_ref, width, out_ref, member, chunk=512):
    experts, _, _ = out_ref.shape
    per_expert = table.shape[1] // experts
    turned = jnp.transpose(table)
    low = member * per_expert
    for c in range(0, width, chunk):
        part = dot_nn(turned, rows_ref[:, c : c + chunk]).astype(BF)
        out_ref[:, low : low + per_expert, c : c + chunk] = part.reshape(
            experts, per_expert, chunk
        )


def first_kernel(n_dp, room, n_shards, *refs):
    x_refs = refs[:n_dp]
    gate_ref, up_ref, g_ref, u_ref, xs = refs[n_dp:]
    experts, expert_rows, width = xs.shape
    n_sorted = experts * expert_rows // n_dp

    @pl.when(pl.program_id(0) == 0)
    def _():
        for d in range(n_dp):
            table = sorted_table(x_refs[d][:, width : width + META], room, n_shards, n_sorted)
            spread(table, x_refs[d], width, xs, d)

    step = gate_ref.shape[0]
    for i in range(step):
        x_block = xs[pl.program_id(0) * step + i]
        g_ref[i] = dot_nt(x_block, gate_ref[i])
        u_ref[i] = dot_nt(x_block, up_ref[i])


def first_layer(x_list, gate, up, room, n_shards):
    n_dp = len(x_list)
    experts, hidden, width = gate.shape
    expert_rows = n_dp * n_shards * MOST
    step = step_of(experts, 4)
    by_expert = lambda e: (e, 0, 0)
    shape = jax.ShapeDtypeStruct((experts, expert_rows, hidden), F32)
    return pl.pallas_call(
        functools.partial(first_kernel, n_dp, room, n_shards),
        grid=(experts // step,),
        in_specs=[whole(x) for x in x_list]
        + [pl.BlockSpec((step, hidden, width), by_expert)] * 2,
        out_specs=[pl.BlockSpec((step, expert_rows, hidden), by_expert)] * 2,
        out_shape=[shape, shape],
        scratch_shapes=[pltpu.VMEM((experts, expert_rows, width), BF)],
        compiler_params=params(big_limit(x_list[0])),
        cost_estimate=cost(2e9, 3e7),
        name="gate_up",
    )(*x_list, gate, up)


def second_kernel(n_dp, room, n_shards, *refs):
    m_refs, c_refs = refs[:n_dp], refs[n_dp : 2 * n_dp]
    g_ref, u_ref, down_ref, dg_ref, du_ref, hw_ref, cs_ref, r_ref, cs, ms = refs[2 * n_dp :]
    experts, expert_rows, width = cs.shape
    n_sorted = experts * expert_rows // n_dp

    @pl.when(pl.program_id(0) == 0)
    def _():
        for d in range(n_dp):
            meta = m_refs[d][...]
            table = sorted_table(meta, room, n_shards, n_sorted)
            spread(table, c_refs[d], width, cs, d)
            spread(table, m_refs[d], META, ms, d, META)

    step = g_ref.shape[0]
    for i in range(step):
        at = pl.program_id(0) * step + i
        c_block = cs[at]
        cs_ref[i] = c_block
        weight = ms[at][:, 1:2].astype(F32)
        back = dot_nt(c_block, down_ref[i])
        g, u = g_ref[i], u_ref[i]
        sig = jax.nn.sigmoid(g)
        act = g * sig
        hidden = act * u
        router = jnp.sum(hidden.astype(BF).astype(F32) * back, axis=1, keepdims=True)
        r_ref[i] = jnp.broadcast_to(router, (expert_rows, META)).astype(BF)
        hw_ref[i] = (hidden * weight).astype(BF)
        scaled = back * weight
        dg_ref[i] = (scaled * u * (sig * (1.0 + g * (1.0 - sig)))).astype(BF)
        du_ref[i] = (scaled * act).astype(BF)


def second_layer(x_list, c_list, g, u, down, room, n_shards):
    n_dp = len(c_list)
    experts, hidden, width = down.shape
    expert_rows = g.shape[1]
    slots = c_list[0].shape[0]
    step = step_of(experts, 4)
    by_expert = lambda e: (e, 0, 0)
    small = jax.ShapeDtypeStruct((experts, expert_rows, hidden), BF)
    small_spec = pl.BlockSpec((step, expert_rows, hidden), by_expert)
    return pl.pallas_call(
        functools.partial(second_kernel, n_dp, room, n_shards),
        grid=(experts // step,),
        in_specs=[pl.BlockSpec((slots, META), lambda e: (0, width // META))] * n_dp
        + [whole(c) for c in c_list]
        + [small_spec] * 2
        + [pl.BlockSpec((step, hidden, width), by_expert)],
        out_specs=[small_spec] * 3
        + [
            pl.BlockSpec((step, expert_rows, width), by_expert),
            pl.BlockSpec((step, expert_rows, META), by_expert),
        ],
        out_shape=[small] * 3
        + [
            jax.ShapeDtypeStruct((experts, expert_rows, width), BF),
            jax.ShapeDtypeStruct((experts, expert_rows, META), BF),
        ],
        scratch_shapes=[
            pltpu.VMEM((experts, expert_rows, width), BF),
            pltpu.VMEM((experts, expert_rows, META), BF),
        ],
        compiler_params=params(big_limit(c_list[0])),
        cost_estimate=cost(2e9, 2e7),
        name="hidden_grads",
    )(*x_list, *c_list, g, u, down)


def third_kernel(n_dp, room, n_shards, with_router, *refs):
    m_refs = refs[:n_dp]
    rest = refs[n_dp:]
    dg_ref, du_ref, gate_ref, up_ref = rest[:4]
    rest = rest[4:]
    if with_router:
        r_ref, rest = rest[0], rest[1:]
    out_refs, acc = rest[:n_dp], rest[n_dp]
    _, experts, per_expert, width = acc.shape
    step, _, part = gate_ref.shape
    for i in range(step):
        at = pl.program_id(0) * step + i
        grad = (dot_nn(dg_ref[i], gate_ref[i]) + dot_nn(du_ref[i], up_ref[i])).astype(BF)
        for d in range(n_dp):
            low = d * per_expert
            acc[d, at, :, :part] = grad[low : low + per_expert]
            if with_router:
                acc[d, at, :, part:] = r_ref[i, low : low + per_expert]

    @pl.when(pl.program_id(0) == pl.num_programs(0) - 1)
    def _():
        for d in range(n_dp):
            table = sorted_table(m_refs[d][...], room, n_shards, experts * per_expert)
            rows = acc[d].reshape(experts * per_expert, width)
            out_refs[d][...] = dot_nn(table, rows).astype(BF)


def third_layer(x_list, dg, du, gate, up, router, half, n_half, room, n_shards):
    n_dp = len(x_list)
    experts, hidden, full = gate.shape
    expert_rows = dg.shape[1]
    slots = x_list[0].shape[0]
    part = full // n_half
    width = part + (0 if router is None else META)
    step = step_of(experts, 4)
    by_expert = lambda e: (e, 0, 0)
    small_spec = pl.BlockSpec((step, expert_rows, hidden), by_expert)
    weight_spec = pl.BlockSpec((step, hidden, part), lambda e: (e, 0, half))
    args = [*x_list, dg, du, gate, up]
    specs = [pl.BlockSpec((slots, META), lambda e: (0, full // META))] * n_dp
    specs += [small_spec] * 2 + [weight_spec] * 2
    if router is not None:
        args.append(router)
        specs.append(pl.BlockSpec((step, expert_rows, META), by_expert))
    return pl.pallas_call(
        functools.partial(third_kernel, n_dp, room, n_shards, router is not None),
        grid=(experts // step,),
        in_specs=specs,
        out_specs=[pl.BlockSpec((slots, width), lambda e: (0, 0))] * n_dp,
        out_shape=[jax.ShapeDtypeStruct((slots, width), BF)] * n_dp,
        scratch_shapes=[pltpu.VMEM((n_dp, experts, expert_rows // n_dp, width), BF)],
        compiler_params=params(),
        cost_estimate=cost(1e9, 1.5e7),
        name="input_grads",
    )(*args)


def down_kernel(*refs):
    hw_ref, cs_ref, out_ref = refs[0], refs[1], refs[-1]
    for i in range(hw_ref.shape[0]):
        out_ref[i] = dot_tn(hw_ref[i], cs_ref[i]).astype(BF)


def down_layer(hw, cs, low, count, sofar=None):
    experts, rows, hidden = hw.shape
    width = cs.shape[2]
    step = step_of(count, 4)
    by_expert = lambda e: (e + low // step, 0, 0)
    more = [] if sofar is None else [sofar]
    return pl.pallas_call(
        down_kernel,
        grid=(count // step,),
        in_specs=[
            pl.BlockSpec((step, rows, hidden), by_expert),
            pl.BlockSpec((step, rows, width), by_expert),
        ]
        + [pl.BlockSpec(memory_space=pl.ANY)] * len(more),
        out_specs=pl.BlockSpec((step, hidden, width), by_expert),
        out_shape=jax.ShapeDtypeStruct((experts, hidden, width), BF),
        input_output_aliases={2: 0} if more else {},
        compiler_params=params(),
        cost_estimate=cost(5e8, 9e6),
        name="down_grads",
    )(hw, cs, *more)


def home_kernel(per_device, room, n_shards, n_half, n_blocks, ids_ref, *refs):
    table, _, _ = slot_table(ids_ref[...], per_device, room, n_shards)
    blocks, (tok_ref, route_ref) = refs[:-2], refs[-2:]
    part = tok_ref.shape[1] // n_half
    size = n_shards * room // n_blocks
    for h in range(n_half):
        total = None
        for k in range(n_blocks):
            term = dot_nn(table[:, k * size : (k + 1) * size], blocks[h * n_blocks + k][...])
            total = term if total is None else total + term
        tok_ref[:, h * part : (h + 1) * part] = total[:, :part].astype(BF)
        if h == 0:
            column = jnp.broadcast_to(total[:, part : part + 1], (total.shape[0],) * 2)
            route_ref[...] = jnp.transpose(column)[0:1].astype(BF)


def home_rows(ids, halves, width, per_device, room, n_shards):
    n_half, n_blocks = len(halves), len(halves[0])
    count = ids.shape[1]
    blocks = [b for half in halves for b in half]
    return pl.pallas_call(
        functools.partial(home_kernel, per_device, room, n_shards, n_half, n_blocks),
        grid=(1,),
        in_specs=[whole(ids)] + [whole(b) for b in blocks],
        out_specs=[
            pl.BlockSpec((count, width), lambda i: (0, 0)),
            pl.BlockSpec((1, count), lambda i: (0, 0)),
        ],
        out_shape=[
            jax.ShapeDtypeStruct((count, width), BF),
            jax.ShapeDtypeStruct((1, count), BF),
        ],
        compiler_params=params(),
        cost_estimate=cost(2e8, 2e6),
        name="home_rows",
    )(ids, *blocks)


def shifted(value, axis, step):
    n = lax.axis_size(axis)
    return lax.ppermute(value, axis, [(i, (i + step) % n) for i in range(n)])


def swapped(value, axis, bit):
    n = lax.axis_size(axis)
    return lax.ppermute(value, axis, [(i, i ^ bit) for i in range(n)])


def after(value, other):
    return lax.optimization_barrier((value, other))[0]


def direct(n_shards):
    return n_shards <= 4


def to_shards(rows, room, n_shards):
    return join_shards(shard_parts(rows, room, n_shards))


def shard_parts(rows, room, n_shards):
    if not direct(n_shards):
        shaped = rows.reshape(n_shards, room, rows.shape[1])
        return [lax.all_to_all(shaped, "expert", 0, 0, tiled=True).reshape(rows.shape)]
    parts = [rows[:room]]
    for k in range(1, n_shards):
        parts.append(shifted(rows[k * room : (k + 1) * room], "expert", k))
    return parts


def join_shards(parts):
    return parts[0] if len(parts) == 1 else jnp.concatenate(parts)


def from_shards(rows, room, n_shards):
    if not direct(n_shards):
        return [to_shards(rows, room, n_shards)]
    parts = [rows[:room]]
    for k in range(1, n_shards):
        parts.append(shifted(rows[k * room : (k + 1) * room], "expert", -k))
    return parts


def dp_bits(n_dp):
    bits, bit = [], 1
    while bit < n_dp:
        bits.append(bit)
        bit *= 2
    return bits


def far_hop(rows, n_dp):
    return swapped(rows, "dp", dp_bits(n_dp)[-1])


def near_hops(rows, n_dp):
    got = [rows]
    for bit in dp_bits(n_dp)[:-1]:
        got = got + [swapped(r, "dp", bit) for r in got]
    return got


def add_rows(a, b):
    return (a.astype(F32) + b.astype(F32)).astype(BF)


def near_sums(parts, n_dp):
    have = dict(enumerate(parts))
    for bit in dp_bits(n_dp)[:-1]:
        left = {}
        for k in sorted(have, reverse=True):
            if k & bit == 0:
                left[k] = add_rows(have[k], swapped(have[k ^ bit], "dp", bit))
        have = left
    return have[0], have[dp_bits(n_dp)[-1]]


def finish(room, ids, near_x, far_x, own_c, gate, up, down):
    n_shards, n_dp = lax.axis_size("expert"), lax.axis_size("dp")
    per_device, width = gate.shape[0], down.shape[2]
    far_c = far_hop(own_c, n_dp)
    x_list = near_x + near_hops(far_x, n_dp)
    g, u = first_layer(x_list, gate, up, room, n_shards)
    c_list = near_hops(own_c, n_dp) + near_hops(after(far_c, g), n_dp)
    dg, du, hw, cs, router = second_layer(x_list, c_list, g, u, down, room, n_shards)
    first = third_layer(x_list, dg, du, gate, up, router, 0, 2, room, n_shards)
    stay_1, go_1 = near_sums(first, n_dp)
    cut = go_1.shape[0] // 2
    come_1 = far_hop(go_1[:cut], n_dp)
    come_1b = far_hop(go_1[cut:], n_dp)
    dg, du = lax.optimization_barrier((dg, du, go_1))[:2]
    second = third_layer(x_list, dg, du, gate, up, None, 1, 2, room, n_shards)
    second = after(second, come_1)
    stay_2, go_2 = near_sums(second, n_dp)
    early = per_device // 2
    down_grad = down_layer(after(hw, go_2), cs, 0, early) if early else None
    come_2 = far_hop(after(go_2, (come_1b, down_grad)), n_dp)
    come_1 = jnp.concatenate([come_1, come_1b])
    home_1 = from_shards(add_rows(stay_1, come_1), room, n_shards)
    down_grad = down_layer(after(hw, go_2), cs, early, per_device - early, down_grad)
    rows_2 = add_rows(stay_2, after(come_2, down_grad))
    home_2 = from_shards(rows_2, room, n_shards)
    token_grad, route = home_rows(ids, [home_1, home_2], width, per_device, room, n_shards)
    return token_grad, route.reshape(-1, 1), down_grad


def exchange(room, ids, tokens, out_grad, route_weight, per_device, n_shards, n_dp):
    send_x, send_c = pack_rows(ids, tokens, out_grad, route_weight, per_device, room, n_shards)
    own_x = join_shards(shard_parts(send_x, room, n_shards))
    send_c, own_x = lax.optimization_barrier((send_c, own_x))
    far_x, near_x = far_hop(own_x, n_dp), near_hops(own_x, n_dp)
    return near_x, far_x, shard_parts(send_c, room, n_shards)


def agreed(flag, n_dp):
    for step in range(1, lax.axis_size("groups")):
        flag = jnp.maximum(flag, shifted(flag, "groups", step))
    for bit in dp_bits(n_dp):
        flag = jnp.maximum(flag, swapped(flag, "dp", bit))
    return flag


def shards(tokens, out_grad, route_weight, expert_ids, gate, up, down):
    n_shards, n_dp = lax.axis_size("expert"), lax.axis_size("dp")
    per_device, width = gate.shape[0], tokens.shape[1]
    most_rows = min(expert_ids.shape[0], per_device * MOST)
    ids, route_weight = expert_ids.reshape(1, -1), route_weight.reshape(1, -1)
    gate, up = jnp.swapaxes(gate, 1, 2), jnp.swapaxes(up, 1, 2)
    usual = most_rows * 5 // 8
    adaptive = direct(n_shards) and usual % 8 == 0 and (n_shards * usual) % 16 == 0
    room = usual if adaptive else most_rows
    args = (ids, tokens, out_grad, route_weight, per_device, n_shards, n_dp)
    near_x, far_x, parts_c = exchange(room, *args)
    if not adaptive:
        return finish(room, ids, near_x, far_x, join_shards(parts_c), gate, up, down)
    meta = near_x[0][:, width : width + META].astype(F32)
    over = jnp.max(meta, axis=0, keepdims=True)
    over = agreed(after(jnp.broadcast_to(over, (8, META)), near_x[-1]), n_dp)
    own_c = join_shards(parts_c)
    far_x, own_c, over = lax.optimization_barrier((far_x, own_c, over))

    def fits(_):
        return finish(room, ids, near_x, far_x, own_c, gate, up, down)

    def full(_):
        full_near, full_far, full_c = exchange(most_rows, *args)
        return finish(most_rows, ids, full_near, full_far, join_shards(full_c), gate, up, down)

    return lax.cond(over[0, OVER] > 0.0, full, fits, 0)


def solution(mesh):
    rows = P(("groups", "expert", "dp"), None)
    in_specs = (
        rows,
        rows,
        rows,
        rows,
        P("expert", None, "dp"),
        P("expert", None, "dp"),
        P("expert", "dp", None),
    )
    out_specs = (rows, rows, P(("groups", "expert"), "dp", None))
    return jax.shard_map(shards, mesh=mesh, in_specs=in_specs, out_specs=out_specs, check_vma=False)
```

```python
import functools

import jax
import jax.numpy as jnp
from jax import lax
from jax.experimental import pallas as pl
from jax.experimental.pallas import tpu as pltpu
from jax.sharding import PartitionSpec as P

MOST = 4
META = 128
OVER = 2
BF = jnp.bfloat16
F32 = jnp.float32
MIB = 1024 * 1024


def dot_nn(a, b):
    return jnp.dot(a, b, preferred_element_type=F32)


def dot_nt(a, b):
    return lax.dot_general(a, b, (((1,), (1,)), ((), ())), preferred_element_type=F32)


def dot_tn(a, b):
    return lax.dot_general(a, b, (((0,), (0,)), ((), ())), preferred_element_type=F32)


def params(mib=18):
    return pltpu.CompilerParams(vmem_limit_bytes=mib * MIB)


def big_limit(rows):
    return 20 + -(-8 * rows.shape[0] * rows.shape[1] * 2 // MIB)


def cost(flops, moved):
    return pl.CostEstimate(flops=int(flops), bytes_accessed=int(moved), transcendentals=0)


def step_of(experts, most):
    step = 1
    while step * 2 <= most and experts % (step * 2) == 0:
        step *= 2
    return step


def whole(array):
    zeros = (0,) * array.ndim
    return pl.BlockSpec(array.shape, lambda *_: zeros)


def route_columns(ids, per_device, n_shards):
    count = ids.shape[1]
    here = lax.axis_index("expert") if direct(n_shards) else 0
    total = n_shards * per_device
    ids = ids - here * per_device
    ids = jnp.where(ids < 0, ids + total, ids)
    down = jnp.broadcast_to(ids.astype(F32), (count, count))
    across = jnp.transpose(down)
    row = lax.broadcasted_iota(jnp.int32, (count, count), 0)
    col = lax.broadcasted_iota(jnp.int32, (count, count), 1)
    earlier = col < row
    inv = 1.0 / per_device
    across_shard = jnp.floor((across + 0.5) * inv)
    same_expert = jnp.where((across == down) & earlier, 1.0, 0.0)
    same_shard = jnp.where(
        (across_shard == jnp.floor((down + 0.5) * inv)) & earlier, 1.0, 0.0
    )
    rank = jnp.sum(same_expert, axis=1, keepdims=True)
    place = jnp.sum(same_shard, axis=1, keepdims=True)
    shard = across_shard[:, 0:1]
    local = across[:, 0:1] - shard * per_device
    return shard, local, rank, place


def slot_table(ids, per_device, room, n_shards):
    shard, local, rank, place = route_columns(ids, per_device, n_shards)
    slot = jnp.where(place < room, shard * room + place, -1.0).astype(jnp.int32)
    lanes = lax.broadcasted_iota(jnp.int32, (ids.shape[1], n_shards * room), 1)
    over = jnp.max(place, axis=0, keepdims=True) >= room
    return jnp.where(lanes == slot, 1.0, 0.0).astype(BF), local * MOST + rank + 1.0, over


def pack_kernel(per_device, room, n_shards, ids_ref, tok_ref, cot_ref, wgt_ref, x_ref, c_ref):
    table, tag, over = slot_table(ids_ref[...], per_device, room, n_shards)
    width = tok_ref.shape[1]
    x_ref[:, :width] = dot_tn(table, tok_ref[...]).astype(BF)
    lane = lax.broadcasted_iota(jnp.int32, (tag.shape[0], META), 1)
    count = tok_ref.shape[0]
    wgt = jnp.transpose(jnp.broadcast_to(wgt_ref[...].astype(F32), (count, count)))[:, 0:1]
    info = jnp.where(lane == 0, tag, jnp.where(lane == 1, wgt, 0.0))
    packed = dot_tn(table, info.astype(BF))
    lane = lax.broadcasted_iota(jnp.int32, packed.shape, 1)
    flag = jnp.broadcast_to(jnp.where(over, 1.0, 0.0), packed.shape)
    x_ref[:, width:] = jnp.where(lane == OVER, flag, packed).astype(BF)
    c_ref[...] = dot_tn(table, cot_ref[...]).astype(BF)


def pack_rows(ids, tokens, out_grad, wgt, per_device, room, n_shards):
    rows, width = n_shards * room, tokens.shape[1]
    args = (ids, tokens, out_grad, wgt)
    return pl.pallas_call(
        functools.partial(pack_kernel, per_device, room, n_shards),
        grid=(1,),
        in_specs=[whole(a) for a in args],
        out_specs=[
            pl.BlockSpec((rows, width + META), lambda i: (0, 0)),
            pl.BlockSpec((rows, width), lambda i: (0, 0)),
        ],
        out_shape=[
            jax.ShapeDtypeStruct((rows, width + META), BF),
            jax.ShapeDtypeStruct((rows, width), BF),
        ],
        compiler_params=params(),
        cost_estimate=cost(4e8, 4e6),
        name="pack_rows",
    )(*args)


def sorted_table(meta, room, n_shards, n_sorted):
    tag = meta[:, 0:1].astype(F32).astype(jnp.int32)
    rows = lax.broadcasted_iota(jnp.int32, tag.shape, 0)
    source = jnp.floor((rows.astype(F32) + 0.5) * (1.0 / room)).astype(jnp.int32)
    at = tag - 1
    local = at // MOST
    dest = local * (n_shards * MOST) + source * MOST + (at - local * MOST)
    dest = jnp.where(tag > 0, dest, -1)
    lanes = lax.broadcasted_iota(jnp.int32, (meta.shape[0], n_sorted), 1)
    return jnp.where(lanes == dest, 1.0, 0.0).astype(BF)


def spread(table, rows_ref, width, out_ref, member, chunk=512):
    experts, _, _ = out_ref.shape
    per_expert = table.shape[1] // experts
    turned = jnp.transpose(table)
    low = member * per_expert
    for c in range(0, width, chunk):
        part = dot_nn(turned, rows_ref[:, c : c + chunk]).astype(BF)
        out_ref[:, low : low + per_expert, c : c + chunk] = part.reshape(
            experts, per_expert, chunk
        )


def first_kernel(n_dp, room, n_shards, *refs):
    x_refs = refs[:n_dp]
    gate_ref, up_ref, g_ref, u_ref, xs = refs[n_dp:]
    experts, expert_rows, width = xs.shape
    n_sorted = experts * expert_rows // n_dp

    @pl.when(pl.program_id(0) == 0)
    def _():
        for d in range(n_dp):
            table = sorted_table(x_refs[d][:, width : width + META], room, n_shards, n_sorted)
            spread(table, x_refs[d], width, xs, d)

    step = gate_ref.shape[0]
    for i in range(step):
        x_block = xs[pl.program_id(0) * step + i]
        g_ref[i] = dot_nt(x_block, gate_ref[i])
        u_ref[i] = dot_nt(x_block, up_ref[i])


def first_layer(x_list, gate, up, room, n_shards):
    n_dp = len(x_list)
    experts, hidden, width = gate.shape
    expert_rows = n_dp * n_shards * MOST
    step = step_of(experts, 4)
    by_expert = lambda e: (e, 0, 0)
    shape = jax.ShapeDtypeStruct((experts, expert_rows, hidden), F32)
    return pl.pallas_call(
        functools.partial(first_kernel, n_dp, room, n_shards),
        grid=(experts // step,),
        in_specs=[whole(x) for x in x_list]
        + [pl.BlockSpec((step, hidden, width), by_expert)] * 2,
        out_specs=[pl.BlockSpec((step, expert_rows, hidden), by_expert)] * 2,
        out_shape=[shape, shape],
        scratch_shapes=[pltpu.VMEM((experts, expert_rows, width), BF)],
        compiler_params=params(big_limit(x_list[0])),
        cost_estimate=cost(2e9, 3e7),
        name="gate_up",
    )(*x_list, gate, up)


def second_kernel(n_dp, room, n_shards, *refs):
    m_refs, c_refs = refs[:n_dp], refs[n_dp : 2 * n_dp]
    g_ref, u_ref, down_ref, dg_ref, du_ref, hw_ref, cs_ref, r_ref, cs, ms = refs[2 * n_dp :]
    experts, expert_rows, width = cs.shape
    n_sorted = experts * expert_rows // n_dp

    @pl.when(pl.program_id(0) == 0)
    def _():
        for d in range(n_dp):
            meta = m_refs[d][...]
            table = sorted_table(meta, room, n_shards, n_sorted)
            spread(table, c_refs[d], width, cs, d)
            spread(table, m_refs[d], META, ms, d, META)

    step = g_ref.shape[0]
    for i in range(step):
        at = pl.program_id(0) * step + i
        c_block = cs[at]
        cs_ref[i] = c_block
        weight = ms[at][:, 1:2].astype(F32)
        back = dot_nt(c_block, down_ref[i])
        g, u = g_ref[i], u_ref[i]
        sig = jax.nn.sigmoid(g)
        act = g * sig
        hidden = act * u
        router = jnp.sum(hidden.astype(BF).astype(F32) * back, axis=1, keepdims=True)
        r_ref[i] = jnp.broadcast_to(router, (expert_rows, META)).astype(BF)
        hw_ref[i] = (hidden * weight).astype(BF)
        scaled = back * weight
        dg_ref[i] = (scaled * u * (sig * (1.0 + g * (1.0 - sig)))).astype(BF)
        du_ref[i] = (scaled * act).astype(BF)


def second_layer(x_list, c_list, g, u, down, room, n_shards):
    n_dp = len(c_list)
    experts, hidden, width = down.shape
    expert_rows = g.shape[1]
    slots = c_list[0].shape[0]
    step = step_of(experts, 4)
    by_expert = lambda e: (e, 0, 0)
    small = jax.ShapeDtypeStruct((experts, expert_rows, hidden), BF)
    small_spec = pl.BlockSpec((step, expert_rows, hidden), by_expert)
    return pl.pallas_call(
        functools.partial(second_kernel, n_dp, room, n_shards),
        grid=(experts // step,),
        in_specs=[pl.BlockSpec((slots, META), lambda e: (0, width // META))] * n_dp
        + [whole(c) for c in c_list]
        + [small_spec] * 2
        + [pl.BlockSpec((step, hidden, width), by_expert)],
        out_specs=[small_spec] * 3
        + [
            pl.BlockSpec((step, expert_rows, width), by_expert),
            pl.BlockSpec((step, expert_rows, META), by_expert),
        ],
        out_shape=[small] * 3
        + [
            jax.ShapeDtypeStruct((experts, expert_rows, width), BF),
            jax.ShapeDtypeStruct((experts, expert_rows, META), BF),
        ],
        scratch_shapes=[
            pltpu.VMEM((experts, expert_rows, width), BF),
            pltpu.VMEM((experts, expert_rows, META), BF),
        ],
        compiler_params=params(big_limit(c_list[0])),
        cost_estimate=cost(2e9, 2e7),
        name="hidden_grads",
    )(*x_list, *c_list, g, u, down)


def third_kernel(n_dp, room, n_shards, with_router, *refs):
    m_refs = refs[:n_dp]
    rest = refs[n_dp:]
    dg_ref, du_ref, gate_ref, up_ref = rest[:4]
    rest = rest[4:]
    if with_router:
        r_ref, rest = rest[0], rest[1:]
    out_refs, acc = rest[:n_dp], rest[n_dp]
    _, experts, per_expert, width = acc.shape
    step, _, part = gate_ref.shape
    for i in range(step):
        at = pl.program_id(0) * step + i
        grad = (dot_nn(dg_ref[i], gate_ref[i]) + dot_nn(du_ref[i], up_ref[i])).astype(BF)
        for d in range(n_dp):
            low = d * per_expert
            acc[d, at, :, :part] = grad[low : low + per_expert]
            if with_router:
                acc[d, at, :, part:] = r_ref[i, low : low + per_expert]

    @pl.when(pl.program_id(0) == pl.num_programs(0) - 1)
    def _():
        for d in range(n_dp):
            table = sorted_table(m_refs[d][...], room, n_shards, experts * per_expert)
            rows = acc[d].reshape(experts * per_expert, width)
            out_refs[d][...] = dot_nn(table, rows).astype(BF)


def third_layer(x_list, dg, du, gate, up, router, half, n_half, room, n_shards):
    n_dp = len(x_list)
    experts, hidden, full = gate.shape
    expert_rows = dg.shape[1]
    slots = x_list[0].shape[0]
    part = full // n_half
    width = part + (0 if router is None else META)
    step = step_of(experts, 4)
    by_expert = lambda e: (e, 0, 0)
    small_spec = pl.BlockSpec((step, expert_rows, hidden), by_expert)
    weight_spec = pl.BlockSpec((step, hidden, part), lambda e: (e, 0, half))
    args = [*x_list, dg, du, gate, up]
    specs = [pl.BlockSpec((slots, META), lambda e: (0, full // META))] * n_dp
    specs += [small_spec] * 2 + [weight_spec] * 2
    if router is not None:
        args.append(router)
        specs.append(pl.BlockSpec((step, expert_rows, META), by_expert))
    return pl.pallas_call(
        functools.partial(third_kernel, n_dp, room, n_shards, router is not None),
        grid=(experts // step,),
        in_specs=specs,
        out_specs=[pl.BlockSpec((slots, width), lambda e: (0, 0))] * n_dp,
        out_shape=[jax.ShapeDtypeStruct((slots, width), BF)] * n_dp,
        scratch_shapes=[pltpu.VMEM((n_dp, experts, expert_rows // n_dp, width), BF)],
        compiler_params=params(),
        cost_estimate=cost(1e9, 1.5e7),
        name="input_grads",
    )(*args)


def down_kernel(*refs):
    hw_ref, cs_ref, out_ref = refs[0], refs[1], refs[-1]
    for i in range(hw_ref.shape[0]):
        out_ref[i] = dot_tn(hw_ref[i], cs_ref[i]).astype(BF)


def down_layer(hw, cs, low, count, sofar=None):
    experts, rows, hidden = hw.shape
    width = cs.shape[2]
    step = step_of(count, 4)
    by_expert = lambda e: (e + low // step, 0, 0)
    more = [] if sofar is None else [sofar]
    return pl.pallas_call(
        down_kernel,
        grid=(count // step,),
        in_specs=[
            pl.BlockSpec((step, rows, hidden), by_expert),
            pl.BlockSpec((step, rows, width), by_expert),
        ]
        + [pl.BlockSpec(memory_space=pl.ANY)] * len(more),
        out_specs=pl.BlockSpec((step, hidden, width), by_expert),
        out_shape=jax.ShapeDtypeStruct((experts, hidden, width), BF),
        input_output_aliases={2: 0} if more else {},
        compiler_params=params(),
        cost_estimate=cost(5e8, 9e6),
        name="down_grads",
    )(hw, cs, *more)


def home_kernel(per_device, room, n_shards, n_half, n_blocks, ids_ref, *refs):
    table, _, _ = slot_table(ids_ref[...], per_device, room, n_shards)
    blocks, (tok_ref, route_ref) = refs[:-2], refs[-2:]
    part = tok_ref.shape[1] // n_half
    size = n_shards * room // n_blocks
    for h in range(n_half):
        total = None
        for k in range(n_blocks):
            term = dot_nn(table[:, k * size : (k + 1) * size], blocks[h * n_blocks + k][...])
            total = term if total is None else total + term
        tok_ref[:, h * part : (h + 1) * part] = total[:, :part].astype(BF)
        if h == 0:
            column = jnp.broadcast_to(total[:, part : part + 1], (total.shape[0],) * 2)
            route_ref[...] = jnp.transpose(column)[0:1].astype(BF)


def home_rows(ids, halves, width, per_device, room, n_shards):
    n_half, n_blocks = len(halves), len(halves[0])
    count = ids.shape[1]
    blocks = [b for half in halves for b in half]
    return pl.pallas_call(
        functools.partial(home_kernel, per_device, room, n_shards, n_half, n_blocks),
        grid=(1,),
        in_specs=[whole(ids)] + [whole(b) for b in blocks],
        out_specs=[
            pl.BlockSpec((count, width), lambda i: (0, 0)),
            pl.BlockSpec((1, count), lambda i: (0, 0)),
        ],
        out_shape=[
            jax.ShapeDtypeStruct((count, width), BF),
            jax.ShapeDtypeStruct((1, count), BF),
        ],
        compiler_params=params(),
        cost_estimate=cost(2e8, 2e6),
        name="home_rows",
    )(ids, *blocks)


def shifted(value, axis, step):
    n = lax.axis_size(axis)
    return lax.ppermute(value, axis, [(i, (i + step) % n) for i in range(n)])


def swapped(value, axis, bit):
    n = lax.axis_size(axis)
    return lax.ppermute(value, axis, [(i, i ^ bit) for i in range(n)])


def after(value, other):
    return lax.optimization_barrier((value, other))[0]


def direct(n_shards):
    return n_shards <= 4


def to_shards(rows, room, n_shards):
    return join_shards(shard_parts(rows, room, n_shards))


def shard_parts(rows, room, n_shards):
    if not direct(n_shards):
        shaped = rows.reshape(n_shards, room, rows.shape[1])
        return [lax.all_to_all(shaped, "expert", 0, 0, tiled=True).reshape(rows.shape)]
    parts = [rows[:room]]
    for k in range(1, n_shards):
        parts.append(shifted(rows[k * room : (k + 1) * room], "expert", k))
    return parts


def join_shards(parts):
    return parts[0] if len(parts) == 1 else jnp.concatenate(parts)


def from_shards(rows, room, n_shards):
    if not direct(n_shards):
        return [to_shards(rows, room, n_shards)]
    parts = [rows[:room]]
    for k in range(1, n_shards):
        parts.append(shifted(rows[k * room : (k + 1) * room], "expert", -k))
    return parts


def dp_bits(n_dp):
    bits, bit = [], 1
    while bit < n_dp:
        bits.append(bit)
        bit *= 2
    return bits


def far_hop(rows, n_dp):
    return swapped(rows, "dp", dp_bits(n_dp)[-1])


def near_hops(rows, n_dp):
    got = [rows]
    for bit in dp_bits(n_dp)[:-1]:
        got = got + [swapped(r, "dp", bit) for r in got]
    return got


def add_rows(a, b):
    return (a.astype(F32) + b.astype(F32)).astype(BF)


def near_sums(parts, n_dp):
    have = dict(enumerate(parts))
    for bit in dp_bits(n_dp)[:-1]:
        left = {}
        for k in sorted(have, reverse=True):
            if k & bit == 0:
                left[k] = add_rows(have[k], swapped(have[k ^ bit], "dp", bit))
        have = left
    return have[0], have[dp_bits(n_dp)[-1]]


def finish(room, ids, near_x, far_x, own_c, gate, up, down):
    n_shards, n_dp = lax.axis_size("expert"), lax.axis_size("dp")
    per_device, width = gate.shape[0], down.shape[2]
    far_c = far_hop(own_c, n_dp)
    x_list = near_x + near_hops(far_x, n_dp)
    g, u = first_layer(x_list, gate, up, room, n_shards)
    c_list = near_hops(own_c, n_dp) + near_hops(after(far_c, g), n_dp)
    dg, du, hw, cs, router = second_layer(x_list, c_list, g, u, down, room, n_shards)
    first = third_layer(x_list, dg, du, gate, up, router, 0, 2, room, n_shards)
    stay_1, go_1 = near_sums(first, n_dp)
    cut = go_1.shape[0] // 2
    come_1 = far_hop(go_1[:cut], n_dp)
    come_1b = far_hop(go_1[cut:], n_dp)
    dg, du = lax.optimization_barrier((dg, du, go_1))[:2]
    second = third_layer(x_list, dg, du, gate, up, None, 1, 2, room, n_shards)
    second = after(second, come_1)
    stay_2, go_2 = near_sums(second, n_dp)
    early = per_device // 2
    down_grad = down_layer(after(hw, go_2), cs, 0, early) if early else None
    come_2 = far_hop(after(go_2, down_grad), n_dp)
    come_1 = jnp.concatenate([come_1, come_1b])
    home_1 = from_shards(add_rows(stay_1, come_1), room, n_shards)
    down_grad = down_layer(after(hw, go_2), cs, early, per_device - early, down_grad)
    rows_2 = add_rows(stay_2, after(come_2, down_grad))
    home_2 = from_shards(rows_2, room, n_shards)
    token_grad, route = home_rows(ids, [home_1, home_2], width, per_device, room, n_shards)
    return token_grad, route.reshape(-1, 1), down_grad


def exchange(room, ids, tokens, out_grad, route_weight, per_device, n_shards, n_dp):
    send_x, send_c = pack_rows(ids, tokens, out_grad, route_weight, per_device, room, n_shards)
    own_x = join_shards(shard_parts(send_x, room, n_shards))
    send_c, own_x = lax.optimization_barrier((send_c, own_x))
    far_x, near_x = far_hop(own_x, n_dp), near_hops(own_x, n_dp)
    return near_x, far_x, shard_parts(send_c, room, n_shards)


def agreed(flag, n_dp):
    for step in range(1, lax.axis_size("groups")):
        flag = jnp.maximum(flag, shifted(flag, "groups", step))
    for bit in dp_bits(n_dp):
        flag = jnp.maximum(flag, swapped(flag, "dp", bit))
    return flag


def shards(tokens, out_grad, route_weight, expert_ids, gate, up, down):
    n_shards, n_dp = lax.axis_size("expert"), lax.axis_size("dp")
    per_device, width = gate.shape[0], tokens.shape[1]
    most_rows = min(expert_ids.shape[0], per_device * MOST)
    ids, route_weight = expert_ids.reshape(1, -1), route_weight.reshape(1, -1)
    gate, up = jnp.swapaxes(gate, 1, 2), jnp.swapaxes(up, 1, 2)
    usual = most_rows * 5 // 8
    adaptive = direct(n_shards) and usual % 8 == 0 and (n_shards * usual) % 16 == 0
    room = usual if adaptive else most_rows
    args = (ids, tokens, out_grad, route_weight, per_device, n_shards, n_dp)
    near_x, far_x, parts_c = exchange(room, *args)
    if not adaptive:
        return finish(room, ids, near_x, far_x, join_shards(parts_c), gate, up, down)
    meta = near_x[0][:, width : width + META].astype(F32)
    over = jnp.max(meta, axis=0, keepdims=True)
    over = agreed(after(jnp.broadcast_to(over, (8, META)), near_x[-1]), n_dp)
    own_c = join_shards(parts_c)
    far_x, own_c, over = lax.optimization_barrier((far_x, own_c, over))

    def fits(_):
        return finish(room, ids, near_x, far_x, own_c, gate, up, down)

    def full(_):
        full_near, full_far, full_c = exchange(most_rows, *args)
        return finish(most_rows, ids, full_near, full_far, join_shards(full_c), gate, up, down)

    return lax.cond(over[0, OVER] > 0.0, full, fits, 0)


def solution(mesh):
    rows = P(("groups", "expert", "dp"), None)
    in_specs = (
        rows,
        rows,
        rows,
        rows,
        P("expert", None, "dp"),
        P("expert", None, "dp"),
        P("expert", "dp", None),
    )
    out_specs = (rows, rows, P(("groups", "expert"), "dp", None))
    return jax.shard_map(shards, mesh=mesh, in_specs=in_specs, out_specs=out_specs, check_vma=False)
```
